512 devices in a mesh: dp: 32 (over y, x, z_hi), fsdp: 16 (over z_lo, core).
Axes of the slice: x: 4, y: 4, z: 16 (z_hi: 2, z_lo: 8; z = z_hi * 8 + z_lo), core: 2. Of those that a mesh axis runs over, the one named last changes fastest.
Arguments:
- hidden: bfloat16 [65536, 8192], P('dp', 'fsdp'), may hold values from -6 to 6
- gain: float32 [8192], P('fsdp'), may hold values from 0.1 to 1.9
- head_weight: bfloat16 [200, 8192], P(None, 'fsdp'), may hold values from -0.0625 to 0.0625
- lengths: int32 [256], replicated, may hold values from 1 to 1024, 65536 in all
- battles: int32 [1024, 2], replicated, may hold values from 0 to 199, all different within a row
Outputs:
- mean_loss: float32 [], replicated
- coef_table: float32 [256, 200], replicated
- grad_hidden: bfloat16 [65536, 8192], P('dp', 'fsdp')
- grad_head: float32 [200, 8192], P(None, 'fsdp')
- grad_gain: float32 [8192], P('fsdp')
The draws below stay inside these ranges and needn't reach their ends.
Inputs may be any that keep to these rules, and one draw needn't show every extreme that they name: The lengths sum to 65536; the longest prompt has exactly 1024 tokens. `battles`: the two models of a battle differ; the winner comes first; every model fights somewhere.
All inputs are finite; a program needn't handle non-finite values.
Results may differ from the reference program's by a relative error of at most 0.0059.
Values may be sent and summed in bfloat16 or wider, within the bound.
A program may use at most 64 MiB of HBM per device.

```python
import math
import jax
import jax.numpy as jnp
import numpy as np
from jax import lax

D = 8192
MODELS = 200
TOKENS = 65536
PROMPTS = 256
MOST_LEN = 1024
BATTLES = 1024


def block_levels(key, extent, split, low, top_value):
    level, own = 1.0, jax.random.fold_in(key, 6)
    for axis_at, parts in split:
        heights = jnp.exp(jax.random.uniform(jax.random.fold_in(own, axis_at), (parts,), jnp.float32, low / len(split), top_value / len(split)))
        level = level * jnp.repeat(heights, extent[axis_at] // parts).reshape([-1 if axis == axis_at else 1 for axis in range(len(extent))])
    return level


def distinct(rng, rows, number_of, top, lift):
    ranking = jax.random.permutation(jax.random.fold_in(rng, 1), number_of)
    boost = ranking
    for power in range(3):
        boost = boost * boost // number_of
    boost = boost * lift // number_of
    tickets = jax.random.randint(jax.random.fold_in(rng, 2), (rows, number_of), 0, 4096) + boost
    fixed_rows = jax.random.permutation(jax.random.fold_in(rng, 3), rows)[jnp.arange(number_of) % rows]
    tickets = jnp.where(jnp.arange(rows)[:, None] == fixed_rows[None, :], 1 << 14, tickets)
    merit = tickets * number_of + jnp.arange(number_of)
    return lax.top_k(merit.astype(jnp.int32), top)[1].astype(jnp.int32)


def profile(count, total, most, slope):
    portions = [(1 << 20) // math.isqrt(rank ** slope) + 1 for rank in range(2, count + 1)]
    rest, given = total - most - (count - 1), [1] * (count - 1)
    while rest > 0:
        movable = [i for i in range(count - 1) if given[i] < most]
        pool, left = sum([portions[i] for i in movable]), rest
        for i in movable:
            more = min(most - given[i], max(1, left * portions[i] // pool), rest)
            given[i] = given[i] + more
            rest = rest - more
    return np.array([most] + given)


def uneven(own_key, amount, total, limit, skew):
    if amount == 2:
        one = jax.random.randint(own_key, (), max(1, total - limit), min(limit, total - 1) + 1)
        return jnp.stack([one, total - one])
    sizes = jnp.asarray(profile(amount, total, limit, skew), jnp.int32)
    pairs = (amount - 1) // 2
    donor, receiver = sizes[1:1 + 2 * pairs:2], sizes[2:2 + 2 * pairs:2]
    room = jnp.minimum(donor - 1, limit - receiver)
    passed = jax.random.randint(jax.random.fold_in(own_key, 1), (pairs,), 0, 1 << 20) % (room + 1)
    sizes = sizes.at[1:1 + 2 * pairs:2].set(donor - passed).at[2:2 + 2 * pairs:2].set(receiver + passed)
    return sizes[jax.random.permutation(jax.random.fold_in(own_key, 2), amount)]


def normal_values(key, shape, width, limit, cuts=(), kind=jnp.bfloat16):
    array = width * jax.random.normal(key, shape, jnp.float32)
    if cuts:
        array = array * block_levels(key, shape, cuts, -0.22, 0.18)
    return jnp.clip(array, -limit, limit).astype(kind)


def setup_inputs(seed: int = 0) -> dict:
    seeds = jax.random.split(jax.random.key(seed), 6)
    return {
        "hidden": normal_values(seeds[0], (TOKENS, D), 1.0, 6.0, ((0, 32), (1, 16))),
        "gain": jnp.clip(1.0 + 0.18 * jax.random.normal(seeds[1], (D,), jnp.float32), 0.1, 1.9),
        "head_weight": normal_values(seeds[2], (MODELS, D), D ** -0.5, 0.0625, ((1, 16),)),
        "lengths": uneven(seeds[3], PROMPTS, TOKENS, MOST_LEN, 2).astype(jnp.int32),
        "battles": distinct(seeds[4], BATTLES, MODELS, 2, 163),
    }


def battle_terms(pooled, lengths, battles):
    coef_table = jnp.log(pooled / lengths.astype(jnp.float32)[:, None])
    per_prompt = battles.shape[0] // lengths.shape[0]
    prompt_of = jnp.arange(battles.shape[0], dtype=jnp.int32) // per_prompt
    win_coef = coef_table[prompt_of, battles[:, 0]]
    lose_coef = coef_table[prompt_of, battles[:, 1]]
    margin = lose_coef - win_coef
    mean_loss = jnp.mean(jax.nn.softplus(margin))
    battle_slope = jax.nn.sigmoid(margin) / battles.shape[0]
    grad_coef = jnp.zeros_like(coef_table).at[prompt_of, battles[:, 1]].add(battle_slope)
    grad_coef = grad_coef.at[prompt_of, battles[:, 0]].add(-battle_slope)
    return (coef_table, mean_loss, grad_coef / pooled)

def reference(hidden, gain, head_weight, lengths, battles):
    hidden_f = hidden.astype(jnp.float32)
    inv_rms = lax.rsqrt(lax.optimization_barrier(jnp.sum(hidden_f * hidden_f, axis=1)) / D + 1e-06)
    normed = (hidden_f * inv_rms[:, None] * gain[None, :]).astype(jnp.bfloat16)
    logits = lax.dot_general(normed, head_weight, (((1,), (1,)), ((), ())), preferred_element_type=jnp.float32)
    exp_logits = jnp.exp(logits)
    ends = jnp.cumsum(lengths).astype(jnp.int32)
    positions = jnp.arange(TOKENS, dtype=jnp.int32)
    prompt_ids = lax.optimization_barrier(jnp.sum((positions[:, None] >= ends[None, :]).astype(jnp.int32), axis=1)).astype(jnp.int32)
    pooled = jax.ops.segment_sum(exp_logits, prompt_ids, num_segments=PROMPTS)
    coef_table, mean_loss, grad_ratio = battle_terms(pooled, lengths, battles)
    grad_logits = (exp_logits * grad_ratio[prompt_ids]).astype(jnp.bfloat16)
    grad_head = lax.dot_general(grad_logits, normed, (((0,), (0,)), ((), ())), preferred_element_type=jnp.float32)
    grad_normed = jnp.dot(grad_logits, head_weight, preferred_element_type=jnp.float32)
    norm_stat = lax.optimization_barrier(jnp.sum(grad_normed * gain[None, :] * hidden_f, axis=1))
    grad_hidden = gain[None, :] * inv_rms[:, None] * grad_normed - hidden_f * (inv_rms ** 3 * norm_stat / D)[:, None]
    grad_gain = lax.optimization_barrier(jnp.sum(grad_normed * hidden_f * inv_rms[:, None], axis=0))
    return (mean_loss, coef_table, grad_hidden.astype(jnp.bfloat16), grad_head, grad_gain)
```

```python
import functools

import jax
import jax.numpy as jnp
from jax import lax
from jax.experimental import pallas as pl
from jax.experimental.pallas import tpu as pltpu
from jax.sharding import PartitionSpec as P

Y, X, ZH, ZL, NC = 4, 4, 2, 8, 2
XY, F, DP = Y * X, ZL * NC, Y * X * ZH
LANES = 128
PAIRS = 4
EPS = 1e-06
MESH = pl.DeviceIdType.MESH
F32, BF16 = jnp.float32, jnp.bfloat16


def nn(a, b):
    return lax.dot_general(a, b, (((1,), (0,)), ((), ())), preferred_element_type=F32)


def nt(a, b):
    return lax.dot_general(a, b, (((1,), (1,)), ((), ())), preferred_element_type=F32)


def tn(a, b):
    return lax.dot_general(a, b, (((0,), (0,)), ((), ())), preferred_element_type=F32)


def split3(x):
    hi = x.astype(BF16).astype(F32)
    mid = (x - hi).astype(BF16).astype(F32)
    return jnp.concatenate([hi, mid, x - hi - mid], axis=0).astype(BF16)


def join3(x):
    rows = x.shape[0] // 3
    return x[:rows] + x[rows : 2 * rows] + x[2 * rows :]


def kernel(
    models, width, n_battles, blk,
    hidden_hbm, gain_hbm, head_hbm, lens_hbm, battles_hbm,
    loss_ref, coef_ref, gh_hbm, ghead_ref, ggain_ref,
    hid, gain_v, head_v, lens_v, bat_v, wp, wpad, members, ids, raw16, out_v,
    s1_send, s1_recv, s2_buf, s3_send, s3_recv, g_t, g_tile, g_send, s4_recv,
    s5_send, s5_recv, ag, c1_recv, c2_send, c2_recv, c_blk, c5_all, c5_sum, c5_other, ctab,
    load_sem, out_sem, s1_ss, s1_rs, s2_ss, s2_rs, s3_ss, s3_rs, s4_ss, s4_rs, s5_ss, s5_rs,
    s6_ss, s6_rs, c1_ss, c1_rs, c2_ss, c2_rs, c5_ss, c5_rs, c5b_ss, c5b_rs, c6_ss, c6_rs,
):
    toks, dl = hid.shape
    prompts = members.shape[1]
    tiles = -(-models // 16)
    slots = c1_recv.shape[0]
    dp = lax.axis_index("dp")
    f = lax.axis_index("fsdp")
    xy, zh = dp // ZH, dp % ZH
    y, x = xy // X, xy % X
    zl, c = f // NC, f % NC
    base = dp * toks

    def fsdp_peer(k):
        return lax.rem(f + k, F)

    def xy_peer(k):
        return lax.rem(y + k // X, Y) * X + lax.rem(x + k % X, X)

    def xy_dev(q):
        return (q * ZH + zh, f)

    zh_dev = (xy * ZH + (1 - zh), f)
    dp_next = (lax.rem(dp + 1, DP), f)
    dp_prev = (lax.rem(dp + DP - 1, DP), f)

    loads = [
        pltpu.make_async_copy(lens_hbm, lens_v, load_sem.at[0]),
        pltpu.make_async_copy(battles_hbm, bat_v, load_sem.at[1]),
        pltpu.make_async_copy(gain_hbm, gain_v, load_sem.at[2]),
        pltpu.make_async_copy(head_hbm, head_v, load_sem.at[3]),
    ]
    n_blk = toks // blk
    for i in range(n_blk):
        rows = pl.ds(i * blk, blk)
        loads.append(pltpu.make_async_copy(hidden_hbm.at[rows], hid.at[rows], load_sem.at[4 + i]))
    for cp in loads:
        cp.start()

    barrier = pltpu.get_barrier_semaphore()
    partners = [(dp, fsdp_peer(k)) for k in range(1, F)]
    partners += [xy_dev(xy_peer(k)) for k in range(1, XY)]
    partners += [zh_dev, dp_next, dp_prev]
    for dev in partners:
        pl.semaphore_signal(barrier, inc=1, device_id=dev, device_id_type=MESH)

    loads[0].wait()
    lens = jnp.broadcast_to(lens_v[...], (8, prompts))
    len_hi = lens // 32
    len_lo = lens - len_hi * 32
    upto = (
        lax.broadcasted_iota(jnp.int32, (prompts, prompts), 0)
        <= lax.broadcasted_iota(jnp.int32, (prompts, prompts), 1)
    ).astype(F32).astype(BF16)
    ends = (32.0 * nn(len_hi.astype(F32).astype(BF16), upto) + nn(len_lo.astype(F32).astype(BF16), upto))[:1]
    ends = ends.astype(jnp.int32)
    lens = lens[:1]
    starts = ends - lens
    lens_f = lens.astype(F32)
    at_prev = ((starts < base) & (ends > base)).astype(F32)
    at_next = ((starts < base + toks) & (ends > base + toks)).astype(F32)
    owned = ((ends > base) & (ends <= base + toks)).astype(F32)
    for i in range(n_blk):
        pos = base + i * blk + lax.broadcasted_iota(jnp.int32, (blk, prompts), 0)
        inside = (pos >= starts) & (pos < ends)
        members[pl.ds(i * blk, blk), :] = inside.astype(F32).astype(BF16)
    loads[1].wait()
    ids[...] = nt(bat_v[...].astype(F32).astype(BF16), members[...])

    loads[2].wait()
    loads[3].wait()
    wide = 16 * tiles
    head_f = head_v[...].astype(F32)
    if wide > models:
        head_f = jnp.concatenate([head_f, jnp.zeros((wide - models, dl), F32)], axis=0)
    wpad[...] = head_f.astype(BF16)
    wp[...] = (head_f * gain_v[...]).astype(BF16)

    model_of = lax.broadcasted_iota(jnp.int32, (wide, LANES), 0).astype(F32)
    ones_l = jnp.ones((8, LANES), BF16)
    for t in range(tiles, slots * NC):
        raw16[t // NC, t % NC] = jnp.zeros((16, toks), BF16)
    for i in range(n_blk):
        loads[4 + i].wait()
        rows = pl.ds(i * blk, blk)
        h = hid[rows, :]
        raw = nt(wp[...], h)
        for t in range(tiles):
            raw16[t // NC, t % NC, :, rows] = raw[16 * t : 16 * t + 16].astype(BF16)
        hf = h.astype(F32)
        sq = hf * hf
        part = sq[:, :LANES]
        for j in range(1, dl // LANES):
            part = part + sq[:, j * LANES : (j + 1) * LANES]
        part_hi = part.astype(BF16)
        part_lo = (part - part_hi.astype(F32)).astype(BF16)
        sumsq = nt(ones_l, part_hi) + nt(ones_l, part_lo)
        for b in range(blk // LANES):
            lanes = slice(b * LANES, (b + 1) * LANES)
            dest = i * (blk // LANES) + b
            block = raw[:, lanes]
            id_blk = ids[:, pl.ds(i * blk + b * LANES, LANES)]
            picked = [
                jnp.sum(jnp.where(model_of == id_blk[j : j + 1], block, 0.0), axis=0, keepdims=True)
                for j in range(2 * PAIRS)
            ]
            s1_send[dest, 0:8, :] = jnp.concatenate(picked, axis=0)
            s1_send[dest, 8:16, :] = sumsq[:, lanes]

    pl.semaphore_wait(barrier, len(partners))

    def remote(src, dst, ss, rs, dev):
        cp = pltpu.make_async_remote_copy(
            src_ref=src, dst_ref=dst, send_sem=ss, recv_sem=rs, device_id=dev, device_id_type=MESH
        )
        cp.start()
        return cp

    s1 = [
        remote(s1_send.at[fsdp_peer(k)], s1_recv.at[k], s1_ss.at[k], s1_rs.at[k], (dp, fsdp_peer(k)))
        for k in range(1, F)
    ]
    c1 = remote(raw16.at[:, 1 - c], c1_recv, c1_ss, c1_rs, (dp, zl * NC + (1 - c)))
    c1.wait()
    for i in range(slots):
        c2_send[i] = (raw16[i, c].astype(F32) + c1_recv[i].astype(F32)).astype(BF16)

    for cp in s1:
        cp.wait_recv()
    acc = s1_send[f]
    for k in range(1, F):
        acc = acc + s1_recv[k]
    inv = lax.rsqrt(acc[8:16] / width + EPS)
    s2_buf[f] = jnp.concatenate([acc[0:8] * inv, inv], axis=0)
    s2 = [
        remote(s2_buf.at[f], s2_buf.at[f], s2_ss.at[k], s2_rs.at[k], (dp, fsdp_peer(k)))
        for k in range(1, F)
    ]

    def c2_copy(k):
        to = lax.rem(zl + k, ZL)
        return to, pltpu.make_async_remote_copy(
            src_ref=c2_send.at[lax.rem(to, slots)], dst_ref=c2_recv.at[k], send_sem=c2_ss.at[k],
            recv_sem=c2_rs.at[k], device_id=(dp, to * NC + c), device_id_type=MESH,
        )

    for k in range(1, ZL):
        to, cp = c2_copy(k)

        @pl.when(to < slots)
        def _():
            cp.start()

    for cp in s2:
        cp.wait_recv()
    logits = jnp.concatenate([s2_buf[r, 0:8, :] for r in range(F)], axis=1)
    inv = jnp.concatenate([s2_buf[r, 8:16, :] for r in range(F)], axis=1)
    exps = jnp.exp(logits)
    pooled = join3(nn(split3(exps), members[...]))

    s3_send[0] = jnp.broadcast_to(jnp.sum(pooled * at_next, axis=1, keepdims=True), (8, LANES))
    s3_send[1] = jnp.broadcast_to(jnp.sum(pooled * at_prev, axis=1, keepdims=True), (8, LANES))
    s3 = [
        remote(s3_send.at[0], s3_recv.at[0], s3_ss.at[0], s3_rs.at[0], dp_next),
        remote(s3_send.at[1], s3_recv.at[1], s3_ss.at[1], s3_rs.at[1], dp_prev),
    ]
    for cp in s3:
        cp.wait_recv()
    spread = [1] * (prompts // LANES)
    from_prev = jnp.concatenate([s3_recv[0] for _ in spread], axis=1)
    from_next = jnp.concatenate([s3_recv[1] for _ in spread], axis=1)
    pooled = pooled + from_prev * at_prev + from_next * at_next
    pooled = jnp.where(pooled > 0.0, pooled, 1.0)
    coef = jnp.log(pooled / lens_f)
    other = jnp.concatenate([coef[PAIRS:], coef[:PAIRS]], axis=0)
    row_of = lax.broadcasted_iota(jnp.int32, (8, prompts), 0)
    sign = jnp.where(row_of < PAIRS, -1.0, 1.0)
    margin = sign * (coef - other)
    softplus = jnp.maximum(margin, 0.0) + jnp.log1p(jnp.exp(-jnp.abs(margin)))
    loss_part = jnp.sum(jnp.where(row_of < PAIRS, softplus * owned, 0.0)) / n_battles
    ratio = sign * (1.0 / (1.0 + jnp.exp(-margin))) / n_battles / pooled
    grads = exps * join3(nt(split3(ratio), members[...]))
    slope = jnp.sum(grads * logits, axis=0, keepdims=True) * inv[:1] * inv[:1] / width
    grads = grads * inv

    for b in range(toks // LANES):
        lanes = slice(b * LANES, (b + 1) * LANES)
        id_blk = ids[:, lanes]
        full = jnp.zeros((wide, LANES), F32)
        for j in range(2 * PAIRS):
            full = full + jnp.where(model_of == id_blk[j : j + 1], grads[j : j + 1, lanes], 0.0)
        g_t[:, lanes] = full.astype(BF16)
    head_part = nn(g_t[...], hid[...])
    for t in range(tiles):
        g_tile[t] = head_part[16 * t : 16 * t + 16]
        g_send[t] = head_part[16 * t : 16 * t + 16].astype(BF16)
    for t in range(tiles, XY):
        g_tile[t] = jnp.zeros((16, dl), F32)
        g_send[t] = jnp.zeros((16, dl), BF16)
    s4 = [
        remote(g_send.at[xy_peer(k)], s4_recv.at[k], s4_ss.at[k], s4_rs.at[k], xy_dev(xy_peer(k)))
        for k in range(1, XY)
    ]

    for k in range(1, ZL):
        to, cp = c2_copy(k)

        @pl.when(zl < slots)
        def _():
            cp.wait_recv()

    c_blk[...] = jnp.zeros((16, prompts), F32)

    @pl.when(zl < slots)
    def _():
        total = c2_send[zl].astype(F32)
        for k in range(1, ZL):
            total = total + c2_recv[k].astype(F32)
        c_blk[...] = join3(nn(split3(jnp.exp(total * inv[:1])), members[...]))

    mine = jnp.where(f == tiles, loss_part, c_blk[...])
    c5_all[xy] = mine
    c5 = [
        remote(c5_all.at[xy], c5_all.at[xy], c5_ss.at[k], c5_rs.at[k], xy_dev(xy_peer(k)))
        for k in range(1, XY)
    ]

    c_rows = lax.broadcasted_iota(jnp.int32, (16, toks), 0)
    slope_hi = slope.astype(BF16).astype(F32)
    slope_lo = slope - slope_hi
    slope3 = jnp.where(c_rows == 0, slope_hi, jnp.where(c_rows == 1, slope_lo, 0.0)).astype(BF16)
    ones_w = jnp.ones((16, dl), BF16)
    outs = []
    for i in range(n_blk):
        rows = pl.ds(i * blk, blk)
        gn = tn(g_t[:, rows], wpad[...])
        cb = tn(slope3[:, i * blk : (i + 1) * blk], ones_w)
        out_v[rows, :] = (gain_v[...] * gn - hid[rows, :].astype(F32) * cb).astype(BF16)
        cp = pltpu.make_async_copy(out_v.at[rows], gh_hbm.at[rows], out_sem.at[i])
        cp.start()
        outs.append(cp)

    for cp in s4:
        cp.wait_recv()
    total = g_tile[xy]
    for k in range(1, XY):
        total = total + s4_recv[k].astype(F32)
    s5_send[...] = total
    s5 = remote(s5_send, s5_recv, s5_ss, s5_rs, zh_dev)

    for cp in c5:
        cp.wait_recv()
    csum = c5_all[0]
    for q in range(1, XY):
        csum = csum + c5_all[q]
    c5_sum[...] = csum
    c5b = remote(c5_sum, c5_other, c5b_ss, c5b_rs, zh_dev)

    s5.wait_recv()
    ag[xy] = (s5_send[...] + s5_recv[...]).astype(BF16)
    s6 = [
        remote(ag.at[xy], ag.at[xy], s6_ss.at[k], s6_rs.at[k], xy_dev(xy_peer(k)))
        for k in range(1, XY)
    ]

    c5b.wait_recv()
    csum = c5_sum[...] + c5_other[...]
    loss_hi = csum.astype(BF16).astype(F32)
    crow = lax.broadcasted_iota(jnp.int32, (16, prompts), 0)
    loss_blk = jnp.where(crow == 0, loss_hi, jnp.where(crow == 1, csum - loss_hi, 0.0))
    coef_blk = jnp.log(csum / lens_f)
    ctab[f] = jnp.where(f == tiles, loss_blk, coef_blk).astype(BF16)
    c6 = [
        remote(ctab.at[f], ctab.at[f], c6_ss.at[k], c6_rs.at[k], (dp, fsdp_peer(k)))
        for k in range(1, F)
    ]

    for cp in s6:
        cp.wait_recv()
    whole = jnp.concatenate([ag[t].astype(F32) for t in range(tiles)], axis=0)
    ghead_ref[...] = (gain_v[...] * whole)[:models]
    ggain_ref[...] = jnp.sum(wpad[...].astype(F32) * whole, axis=0, keepdims=True)

    for cp in c6:
        cp.wait_recv()
    table = jnp.concatenate([ctab[t].astype(F32) for t in range(tiles)], axis=0)
    coef_ref[...] = jnp.transpose(table)[:, :models]
    loss_ref[0, 0] = jnp.sum(ctab[tiles].astype(F32)[0:2, 0:1])

    for cp in s1 + [c for c in s2] + s3 + s4 + [s5] + s6 + c5 + [c5b] + c6:
        cp.wait_send()
    for k in range(1, ZL):
        to, cp = c2_copy(k)

        @pl.when(to < slots)
        def _():
            cp.wait_send()

    for cp in outs:
        cp.wait()


def on_device(hidden, gain, head_weight, lengths, battles):
    toks, dl = hidden.shape
    models = head_weight.shape[0]
    prompts = lengths.shape[0]
    n_battles = battles.shape[0]
    tiles = -(-models // 16)
    wide = 16 * tiles
    slots = -(-tiles // NC)
    blk = min(512, toks)
    sem = pltpu.SemaphoreType.DMA
    rows8 = battles.reshape(prompts, PAIRS, 2).transpose(2, 1, 0).reshape(2 * PAIRS, prompts)
    vmem = pl.BlockSpec(memory_space=pltpu.VMEM)
    smem = pl.BlockSpec(memory_space=pltpu.SMEM)
    hbm = pl.BlockSpec(memory_space=pl.ANY)
    V = pltpu.VMEM
    loss, coef, gh, ghead, ggain = pl.pallas_call(
        functools.partial(kernel, models, float(dl * F), float(n_battles), blk),
        out_shape=(
            jax.ShapeDtypeStruct((1, 1), F32),
            jax.ShapeDtypeStruct((prompts, models), F32),
            jax.ShapeDtypeStruct((toks, dl), BF16),
            jax.ShapeDtypeStruct((models, dl), F32),
            jax.ShapeDtypeStruct((1, dl), F32),
        ),
        in_specs=[hbm] * 5,
        out_specs=(smem, vmem, hbm, vmem, vmem),
        scratch_shapes=[
            V((toks, dl), BF16), V((1, dl), F32), V((models, dl), BF16),
            V((1, prompts), jnp.int32), V((2 * PAIRS, prompts), jnp.int32),
            V((wide, dl), BF16), V((wide, dl), BF16),
            V((toks, prompts), BF16), V((2 * PAIRS, toks), F32),
            V((slots, NC, 16, toks), BF16), V((toks, dl), BF16),
            V((F, 16, LANES), F32), V((F, 16, LANES), F32), V((F, 16, LANES), F32),
            V((2, 8, LANES), F32), V((2, 8, LANES), F32),
            V((wide, toks), BF16), V((XY, 16, dl), F32), V((XY, 16, dl), BF16),
            V((XY, 16, dl), BF16), V((16, dl), F32), V((16, dl), F32), V((XY, 16, dl), BF16),
            V((slots, 16, toks), BF16), V((slots, 16, toks), BF16), V((ZL, 16, toks), BF16),
            V((16, prompts), F32), V((XY, 16, prompts), F32), V((16, prompts), F32),
            V((16, prompts), F32), V((F, 16, prompts), BF16),
            sem((4 + toks // blk,)), sem((toks // blk,)),
            sem((F,)), sem((F,)), sem((F,)), sem((F,)), sem((2,)), sem((2,)),
            sem((XY,)), sem((XY,)), sem, sem, sem((XY,)), sem((XY,)),
            sem, sem, sem((ZL,)), sem((ZL,)), sem((XY,)), sem((XY,)), sem, sem,
            sem((F,)), sem((F,)),
        ],
        compiler_params=pltpu.CompilerParams(
            collective_id=0, has_side_effects=True, vmem_limit_bytes=48 * 2**20
        ),
        name="head",
    )(hidden, gain.reshape(1, dl), head_weight, lengths.reshape(1, prompts), rows8)
    return loss.reshape(()), coef, gh, ghead, ggain.reshape(dl)


def solution(mesh):
    placed = (P("dp", "fsdp"), P("fsdp"), P(None, "fsdp"), P(), P())
    return jax.shard_map(
        on_device,
        mesh=mesh,
        in_specs=placed,
        out_specs=(P(), P(), P("dp", "fsdp"), P(None, "fsdp"), P("fsdp")),
        check_vma=False,
    )
```

```python
import functools

import jax
import jax.numpy as jnp
from jax import lax
from jax.experimental import pallas as pl
from jax.experimental.pallas import tpu as pltpu
from jax.sharding import PartitionSpec as P

Y, X, ZH, ZL, NC = 4, 4, 2, 8, 2
XY, F, DP = Y * X, ZL * NC, Y * X * ZH
LANES = 128
PAIRS = 4
EPS = 1e-06
MESH = pl.DeviceIdType.MESH
F32, BF16 = jnp.float32, jnp.bfloat16


def nn(a, b):
    return lax.dot_general(a, b, (((1,), (0,)), ((), ())), preferred_element_type=F32)


def nt(a, b):
    return lax.dot_general(a, b, (((1,), (1,)), ((), ())), preferred_element_type=F32)


def tn(a, b):
    return lax.dot_general(a, b, (((0,), (0,)), ((), ())), preferred_element_type=F32)


def split3(x):
    hi = x.astype(BF16).astype(F32)
    mid = (x - hi).astype(BF16).astype(F32)
    return jnp.concatenate([hi, mid, x - hi - mid], axis=0).astype(BF16)


def join3(x):
    rows = x.shape[0] // 3
    return x[:rows] + x[rows : 2 * rows] + x[2 * rows :]


def kernel(
    models, width, n_battles, blk,
    hidden_hbm, gain_hbm, head_hbm, lens_hbm, battles_hbm,
    loss_ref, coef_ref, gh_hbm, ghead_ref, ggain_ref,
    hid, gain_v, head_v, lens_v, bat_v, wp, wpad, members, ids, raw16, out_v,
    q_send, q_recv, i_buf, s1_send, s1_recv, s2_buf, s3_send, s3_recv, g_t, g_tile, g_send, s4_recv,
    s5_send, s5_recv, ag, c1_recv, c5_all, c5_sum, c5_other, ctab,
    load_sem, out_sem, q_ss, q_rs, i_ss, i_rs, s1_ss, s1_rs, s2_ss, s2_rs, s3_ss, s3_rs, s4_ss, s4_rs,
    s5_ss, s5_rs, s6_ss, s6_rs, c1_ss, c1_rs, c2_ss, c2_rs, c5_ss, c5_rs, c5b_ss, c5b_rs, c6_ss, c6_rs, *halves,
):
    toks, dl = hid.shape
    prompts = members.shape[1]
    tiles = -(-models // 16)
    levels = len(halves) // 2
    half, half_recv = halves[:levels], halves[levels:]
    dp = lax.axis_index("dp")
    f = lax.axis_index("fsdp")
    xy, zh = dp // ZH, dp % ZH
    y, x = xy // X, xy % X
    zl, c = f // NC, f % NC
    base = dp * toks

    def fsdp_peer(k):
        return lax.rem(f + k, F)

    def xy_peer(k):
        return lax.rem(y + k // X, Y) * X + lax.rem(x + k % X, X)

    def xy_dev(q):
        return (q * ZH + zh, f)

    zh_dev = (xy * ZH + (1 - zh), f)
    dp_next = (lax.rem(dp + 1, DP), f)
    dp_prev = (lax.rem(dp + DP - 1, DP), f)

    loads = [
        pltpu.make_async_copy(lens_hbm, lens_v, load_sem.at[0]),
        pltpu.make_async_copy(battles_hbm, bat_v, load_sem.at[1]),
        pltpu.make_async_copy(gain_hbm, gain_v, load_sem.at[2]),
        pltpu.make_async_copy(head_hbm, head_v, load_sem.at[3]),
    ]
    n_blk = toks // blk
    for i in range(n_blk):
        rows = pl.ds(i * blk, blk)
        loads.append(pltpu.make_async_copy(hidden_hbm.at[rows], hid.at[rows], load_sem.at[4 + i]))
    for cp in loads:
        cp.start()

    barrier = pltpu.get_barrier_semaphore()
    partners = [(dp, fsdp_peer(k)) for k in range(1, F)]
    partners += [xy_dev(xy_peer(k)) for k in range(1, XY)]
    partners += [zh_dev, dp_next, dp_prev]
    for dev in partners:
        pl.semaphore_signal(barrier, inc=1, device_id=dev, device_id_type=MESH)

    loads[0].wait()
    lens = jnp.broadcast_to(lens_v[...], (8, prompts))
    len_hi = lens // 32
    len_lo = lens - len_hi * 32
    upto = (
        lax.broadcasted_iota(jnp.int32, (prompts, prompts), 0)
        <= lax.broadcasted_iota(jnp.int32, (prompts, prompts), 1)
    ).astype(F32).astype(BF16)
    ends = (32.0 * nn(len_hi.astype(F32).astype(BF16), upto) + nn(len_lo.astype(F32).astype(BF16), upto))[:1]
    ends = ends.astype(jnp.int32)
    lens = lens[:1]
    starts = ends - lens
    lens_f = lens.astype(F32)
    at_prev = ((starts < base) & (ends > base)).astype(F32)
    at_next = ((starts < base + toks) & (ends > base + toks)).astype(F32)
    owned = ((ends > base) & (ends <= base + toks)).astype(F32)
    for i in range(n_blk):
        pos = base + i * blk + lax.broadcasted_iota(jnp.int32, (blk, prompts), 0)
        inside = (pos >= starts) & (pos < ends)
        members[pl.ds(i * blk, blk), :] = inside.astype(F32).astype(BF16)
    loads[1].wait()
    n_bat = bat_v.shape[1]
    bat_row = lax.broadcasted_iota(jnp.int32, (2 * PAIRS, n_bat), 0)
    bat_lane = lax.broadcasted_iota(jnp.int32, (2 * PAIRS, n_bat), 1)
    bat = jnp.where(bat_row < PAIRS, bat_v[0:1, :], bat_v[1:2, :])
    bat = jnp.where(bat_lane % PAIRS == bat_row % PAIRS, bat, 0)
    judged = lax.broadcasted_iota(jnp.int32, (n_bat, prompts), 0) // PAIRS
    judged = judged == lax.broadcasted_iota(jnp.int32, (n_bat, prompts), 1)
    bat = nn(bat.astype(F32).astype(BF16), judged.astype(F32).astype(BF16))
    ids[...] = nt(bat.astype(BF16), members[...])

    loads[2].wait()
    loads[3].wait()
    wide = 16 * tiles
    head_f = head_v[...].astype(F32)
    if wide > models:
        head_f = jnp.concatenate([head_f, jnp.zeros((wide - models, dl), F32)], axis=0)
    wpad[...] = head_f.astype(BF16)
    wp[...] = (head_f * gain_v[...]).astype(BF16)

    def remote(src, dst, ss, rs, dev):
        cp = pltpu.make_async_remote_copy(
            src_ref=src, dst_ref=dst, send_sem=ss, recv_sem=rs, device_id=dev, device_id_type=MESH
        )
        cp.start()
        return cp

    ones_l = jnp.ones((8, LANES), BF16)
    for i in range(n_blk):
        loads[4 + i].wait()
        hf = hid[pl.ds(i * blk, blk), :].astype(F32)
        sq = hf * hf
        part = sq[:, :LANES]
        for j in range(1, dl // LANES):
            part = part + sq[:, j * LANES : (j + 1) * LANES]
        part_hi = part.astype(BF16)
        part_lo = (part - part_hi.astype(F32)).astype(BF16)
        sumsq = nt(ones_l, part_hi) + nt(ones_l, part_lo)
        for b in range(blk // LANES):
            q_send[i * (blk // LANES) + b] = sumsq[0:1, b * LANES : (b + 1) * LANES]
    pl.semaphore_wait(barrier, len(partners))
    q_cp = [
        remote(q_send.at[fsdp_peer(k)], q_recv.at[k], q_ss.at[k], q_rs.at[k], (dp, fsdp_peer(k)))
        for k in range(1, F)
    ]

    model_of = lax.broadcasted_iota(jnp.int32, (wide, LANES), 0).astype(F32)
    for t in range(tiles, ZL * NC):
        raw16[t // NC, t % NC] = jnp.zeros((16, toks), BF16)
    for i in range(n_blk):
        rows = pl.ds(i * blk, blk)
        raw = nt(wp[...], hid[rows, :])
        for t in range(tiles):
            raw16[t // NC, t % NC, :, rows] = raw[16 * t : 16 * t + 16].astype(BF16)
        for b in range(blk // LANES):
            lanes = slice(b * LANES, (b + 1) * LANES)
            block = raw[:, lanes]
            id_blk = ids[:, pl.ds(i * blk + b * LANES, LANES)]
            picked = [
                jnp.sum(jnp.where(model_of == id_blk[j : j + 1], block, 0.0), axis=0, keepdims=True)
                for j in range(2 * PAIRS)
            ]
            s1_send[i * (blk // LANES) + b] = jnp.concatenate(picked, axis=0)

    s1 = [
        remote(s1_send.at[fsdp_peer(k)], s1_recv.at[k], s1_ss.at[k], s1_rs.at[k], (dp, fsdp_peer(k)))
        for k in range(1, F)
    ]
    c1 = remote(raw16.at[:, 1 - c], c1_recv, c1_ss, c1_rs, (dp, zl * NC + (1 - c)))
    for cp in q_cp:
        cp.wait_recv()
    acc = q_send[f]
    for k in range(1, F):
        acc = acc + q_recv[k]
    inv_own = lax.rsqrt(acc / width + EPS)
    i_buf[f] = inv_own
    i_cp = [
        remote(i_buf.at[f], i_buf.at[f], i_ss.at[k], i_rs.at[k], (dp, fsdp_peer(k)))
        for k in range(1, F)
    ]

    bits = [(zl >> n) % 2 for n in range(levels)]

    def halve(n):
        step = 1 << n
        peer = (zl + step - 2 * step * bits[n]) * NC + c
        return remote(half[n].at[:, 1 - bits[n]], half_recv[n], c2_ss.at[n], c2_rs.at[n], (dp, peer))

    def fold(n):
        for j in range(half_recv[n].shape[0]):
            total = half[n][j, bits[n]].astype(F32) + half_recv[n][j].astype(F32)
            half[n + 1][j // 2, j % 2] = total.astype(BF16)

    c1.wait_recv()
    for k in range(ZL):
        half[0][k // 2, k % 2] = (raw16[k, c].astype(F32) + c1_recv[k].astype(F32)).astype(BF16)
    c2 = [halve(0)]

    for cp in s1:
        cp.wait_recv()
    acc = s1_send[f]
    for k in range(1, F):
        acc = acc + s1_recv[k]
    s2_buf[f] = acc * inv_own
    s2 = [
        remote(s2_buf.at[f], s2_buf.at[f], s2_ss.at[k], s2_rs.at[k], (dp, fsdp_peer(k)))
        for k in range(1, F)
    ]
    for n in range(0, levels - 1)[:1]:
        c2[n].wait_recv()
        fold(n)
        c2.append(halve(n + 1))

    for cp in i_cp + s2:
        cp.wait_recv()
    logits = jnp.concatenate([s2_buf[r] for r in range(F)], axis=1)
    inv = jnp.concatenate([i_buf[r] for r in range(F)], axis=1)
    exps = jnp.exp(logits)
    pooled = join3(nn(split3(exps), members[...]))

    s3_send[0] = jnp.broadcast_to(jnp.sum(pooled * at_next, axis=1, keepdims=True), (8, LANES))
    s3_send[1] = jnp.broadcast_to(jnp.sum(pooled * at_prev, axis=1, keepdims=True), (8, LANES))
    s3 = [
        remote(s3_send.at[0], s3_recv.at[0], s3_ss.at[0], s3_rs.at[0], dp_next),
        remote(s3_send.at[1], s3_recv.at[1], s3_ss.at[1], s3_rs.at[1], dp_prev),
    ]
    for n in range(0, levels - 1)[1:]:
        c2[n].wait_recv()
        fold(n)
        c2.append(halve(n + 1))
    for cp in s3:
        cp.wait_recv()
    spread = [1] * (prompts // LANES)
    from_prev = jnp.concatenate([s3_recv[0] for _ in spread], axis=1)
    from_next = jnp.concatenate([s3_recv[1] for _ in spread], axis=1)
    pooled = pooled + from_prev * at_prev + from_next * at_next
    pooled = jnp.where(pooled > 0.0, pooled, 1.0)
    coef = jnp.log(pooled / lens_f)
    other = jnp.concatenate([coef[PAIRS:], coef[:PAIRS]], axis=0)
    row_of = lax.broadcasted_iota(jnp.int32, (8, prompts), 0)
    sign = jnp.where(row_of < PAIRS, -1.0, 1.0)
    margin = sign * (coef - other)
    softplus = jnp.maximum(margin, 0.0) + jnp.log1p(jnp.exp(-jnp.abs(margin)))
    loss_part = jnp.sum(jnp.where(row_of < PAIRS, softplus * owned, 0.0)) / n_battles
    ratio = sign * (1.0 / (1.0 + jnp.exp(-margin))) / n_battles / pooled
    grads = exps * join3(nt(split3(ratio), members[...]))
    slope = jnp.sum(grads * logits, axis=0, keepdims=True) * inv * inv / width
    grads = grads * inv

    for b in range(toks // LANES):
        lanes = slice(b * LANES, (b + 1) * LANES)
        id_blk = ids[:, lanes]
        full = jnp.zeros((wide, LANES), F32)
        for j in range(2 * PAIRS):
            full = full + jnp.where(model_of == id_blk[j : j + 1], grads[j : j + 1, lanes], 0.0)
        g_t[:, lanes] = full.astype(BF16)
    head_part = nn(g_t[...], hid[...])
    for t in range(tiles):
        g_tile[t] = head_part[16 * t : 16 * t + 16]
        g_send[t] = head_part[16 * t : 16 * t + 16].astype(BF16)
    for t in range(tiles, XY):
        g_tile[t] = jnp.zeros((16, dl), F32)
        g_send[t] = jnp.zeros((16, dl), BF16)
    s4 = [
        remote(g_send.at[xy_peer(k)], s4_recv.at[k], s4_ss.at[k], s4_rs.at[k], xy_dev(xy_peer(k)))
        for k in range(1, XY)
    ]

    c2[-1].wait_recv()
    tile = half[-1][0, bits[-1]].astype(F32) + half_recv[-1][0].astype(F32)
    c_blk = join3(nn(split3(jnp.exp(tile * inv)), members[...]))
    mine = jnp.where(f == tiles, loss_part, c_blk)
    c5_all[xy] = mine
    c5 = [
        remote(c5_all.at[xy], c5_all.at[xy], c5_ss.at[k], c5_rs.at[k], xy_dev(xy_peer(k)))
        for k in range(1, XY)
    ]

    c_rows = lax.broadcasted_iota(jnp.int32, (16, toks), 0)
    slope_hi = slope.astype(BF16).astype(F32)
    slope_lo = slope - slope_hi
    slope3 = jnp.where(c_rows == 0, slope_hi, jnp.where(c_rows == 1, slope_lo, 0.0)).astype(BF16)
    ones_w = jnp.ones((16, dl), BF16)
    outs = []
    for i in range(n_blk):
        rows = pl.ds(i * blk, blk)
        gn = tn(g_t[:, rows], wpad[...])
        cb = tn(slope3[:, i * blk : (i + 1) * blk], ones_w)
        out_v[rows, :] = (gain_v[...] * gn - hid[rows, :].astype(F32) * cb).astype(BF16)
        cp = pltpu.make_async_copy(out_v.at[rows], gh_hbm.at[rows], out_sem.at[i])
        cp.start()
        outs.append(cp)

    for cp in s4:
        cp.wait_recv()
    total = g_tile[xy]
    for k in range(1, XY):
        total = total + s4_recv[k].astype(F32)
    s5_send[...] = total
    s5 = remote(s5_send, s5_recv, s5_ss, s5_rs, zh_dev)

    for cp in c5:
        cp.wait_recv()
    csum = c5_all[0]
    for q in range(1, XY):
        csum = csum + c5_all[q]
    c5_sum[...] = csum
    c5b = remote(c5_sum, c5_other, c5b_ss, c5b_rs, zh_dev)

    s5.wait_recv()
    ag[xy] = (s5_send[...] + s5_recv[...]).astype(BF16)
    s6 = [
        remote(ag.at[xy], ag.at[xy], s6_ss.at[k], s6_rs.at[k], xy_dev(xy_peer(k)))
        for k in range(1, XY)
    ]

    c5b.wait_recv()
    csum = c5_sum[...] + c5_other[...]
    loss_hi = csum.astype(BF16).astype(F32)
    crow = lax.broadcasted_iota(jnp.int32, (16, prompts), 0)
    loss_blk = jnp.where(crow == 0, loss_hi, jnp.where(crow == 1, csum - loss_hi, 0.0))
    coef_blk = jnp.log(csum / lens_f)
    ctab[f] = jnp.where(f == tiles, loss_blk, coef_blk).astype(BF16)
    c6 = [
        remote(ctab.at[f], ctab.at[f], c6_ss.at[k], c6_rs.at[k], (dp, fsdp_peer(k)))
        for k in range(1, F)
    ]

    for cp in s6:
        cp.wait_recv()
    whole = jnp.concatenate([ag[t].astype(F32) for t in range(tiles)], axis=0)
    ghead_ref[...] = (gain_v[...] * whole)[:models]
    ggain_ref[...] = jnp.sum(wpad[...].astype(F32) * whole, axis=0, keepdims=True)

    for cp in c6:
        cp.wait_recv()
    table = jnp.concatenate([ctab[t].astype(F32) for t in range(tiles)], axis=0)
    coef_ref[...] = table[:models]
    loss_ref[0, 0] = jnp.sum(ctab[tiles].astype(F32)[0:2, 0:1])

    for cp in q_cp + i_cp + s1 + s2 + s3 + s4 + [s5] + s6 + [c1] + c2 + c5 + [c5b] + c6:
        cp.wait_send()
    for cp in outs:
        cp.wait()


def hand_out(loss, coef, gh, ghead, ggain, loss_o, coef_o, gh_o, ghead_o, ggain_o, sems):
    rows = gh.shape[0] // 4
    pairs = [(gh.at[pl.ds(n * rows, rows)], gh_o.at[pl.ds(n * rows, rows)]) for n in range(4)]
    pairs += [(ghead, ghead_o), (coef, coef_o), (ggain, ggain_o)]
    cps = [pltpu.make_async_copy(a, b, sems.at[n]) for n, (a, b) in enumerate(pairs)]
    for cp in cps:
        cp.start()
    loss_o[0, 0] = loss[0, 0]
    for cp in cps:
        cp.wait()


def on_device(hidden, gain, head_weight, lengths, battles):
    toks, dl = hidden.shape
    models = head_weight.shape[0]
    prompts = lengths.shape[0]
    n_battles = battles.shape[0]
    tiles = -(-models // 16)
    wide = 16 * tiles
    blk = min(512, toks)
    levels = ZL.bit_length() - 1
    sem = pltpu.SemaphoreType.DMA
    vmem = pl.BlockSpec(memory_space=pltpu.VMEM)
    smem = pl.BlockSpec(memory_space=pltpu.SMEM)
    hbm = pl.BlockSpec(memory_space=pl.ANY)
    V = pltpu.VMEM
    shapes = (
        jax.ShapeDtypeStruct((1, 1), F32),
        jax.ShapeDtypeStruct((models, prompts), F32),
        jax.ShapeDtypeStruct((toks, dl), BF16),
        jax.ShapeDtypeStruct((models, dl), F32),
        jax.ShapeDtypeStruct((1, dl), F32),
    )
    results = pl.pallas_call(
        functools.partial(kernel, models, float(dl * F), float(n_battles), blk),
        out_shape=shapes,
        in_specs=[hbm] * 5,
        out_specs=(smem, vmem, hbm, vmem, vmem),
        scratch_shapes=[
            V((toks, dl), BF16), V((1, dl), F32), V((models, dl), BF16),
            V((1, prompts), jnp.int32), V((2, n_battles), jnp.int32),
            V((wide, dl), BF16), V((wide, dl), BF16),
            V((toks, prompts), BF16), V((2 * PAIRS, toks), F32),
            V((ZL, NC, 16, toks), BF16), V((toks, dl), BF16),
            V((F, 1, LANES), F32), V((F, 1, LANES), F32), V((F, 1, LANES), F32),
            V((F, 8, LANES), F32), V((F, 8, LANES), F32), V((F, 8, LANES), F32),
            V((2, 8, LANES), F32), V((2, 8, LANES), F32),
            V((wide, toks), BF16), V((XY, 16, dl), F32), V((XY, 16, dl), BF16),
            V((XY, 16, dl), BF16), V((16, dl), F32), V((16, dl), F32), V((XY, 16, dl), BF16),
            V((ZL, 16, toks), BF16),
            V((XY, 16, prompts), F32), V((16, prompts), F32), V((16, prompts), F32),
            V((F, 16, prompts), BF16),
            sem((4 + toks // blk,)), sem((toks // blk,)),
            sem((F,)), sem((F,)), sem((F,)), sem((F,)),
            sem((F,)), sem((F,)), sem((F,)), sem((F,)), sem((2,)), sem((2,)),
            sem((XY,)), sem((XY,)), sem, sem, sem((XY,)), sem((XY,)),
            sem, sem, sem((levels,)), sem((levels,)), sem((XY,)), sem((XY,)), sem, sem,
            sem((F,)), sem((F,)),
        ]
        + [V((ZL >> (n + 1), 2, 16, toks), BF16) for n in range(levels)]
        + [V((ZL >> (n + 1), 16, toks), BF16) for n in range(levels)],
        compiler_params=pltpu.CompilerParams(
            collective_id=0, has_side_effects=True, vmem_limit_bytes=60 * 2**20
        ),
        name="head",
    )(hidden, gain.reshape(1, dl), head_weight, lengths.reshape(1, prompts), battles.T)
    loss, coef, gh, ghead, ggain = pl.pallas_call(
        hand_out,
        out_shape=shapes,
        in_specs=[smem] + [hbm] * 4,
        out_specs=(smem,) + (hbm,) * 4,
        scratch_shapes=[sem((7,))],
        compiler_params=pltpu.CompilerParams(vmem_limit_bytes=60 * 2**20),
        name="hand_out",
    )(*results)
    return loss.reshape(()), coef.T, gh, ghead, ggain.reshape(dl)


def solution(mesh):
    placed = (P("dp", "fsdp"), P("fsdp"), P(None, "fsdp"), P(), P())
    return jax.shard_map(
        on_device,
        mesh=mesh,
        in_specs=placed,
        out_specs=(P(), P(), P("dp", "fsdp"), P(None, "fsdp"), P("fsdp")),
        check_vma=False,
    )
```

```python
import functools

import jax
import jax.numpy as jnp
from jax import lax
from jax.experimental import pallas as pl
from jax.experimental.pallas import tpu as pltpu
from jax.sharding import PartitionSpec as P

Y, X, ZH, ZL, NC = 4, 4, 2, 8, 2
XY, F, DP = Y * X, ZL * NC, Y * X * ZH
LANES = 128
PAIRS = 4
EPS = 1e-06
MESH = pl.DeviceIdType.MESH
F32, BF16 = jnp.float32, jnp.bfloat16


def nn(a, b):
    return lax.dot_general(a, b, (((1,), (0,)), ((), ())), preferred_element_type=F32)


def nt(a, b):
    return lax.dot_general(a, b, (((1,), (1,)), ((), ())), preferred_element_type=F32)


def tn(a, b):
    return lax.dot_general(a, b, (((0,), (0,)), ((), ())), preferred_element_type=F32)


def split3(x):
    hi = x.astype(BF16).astype(F32)
    mid = (x - hi).astype(BF16).astype(F32)
    return jnp.concatenate([hi, mid, x - hi - mid], axis=0).astype(BF16)


def join3(x):
    rows = x.shape[0] // 3
    return x[:rows] + x[rows : 2 * rows] + x[2 * rows :]


def kernel(
    models, width, n_battles, blk,
    hidden_hbm, gain_hbm, head_hbm, lens_hbm, battles_hbm,
    loss_ref, coef_ref, gh_hbm, ghead_ref, ggain_ref,
    hid, gain_v, head_v, lens_v, bat_v, wp, wpad, members, ids, raw, raw16, out_v,
    q_send, q_recv, i_buf, s1_send, s1_recv, s2_buf, b_send, b_recv, g_t, g_tile, g_send, s4_recv,
    s5_send, s5_recv, ag, c1_recv, c5_all, c5_sum, c5_other, ctab,
    load_sem, out_sem, q_ss, q_rs, i_ss, i_rs, s1_ss, s1_rs, s2_ss, s2_rs, b_ss, b_rs, s4_ss, s4_rs,
    s5_ss, s5_rs, s6_ss, s6_rs, c1_ss, c1_rs, c2_ss, c2_rs, c5_ss, c5_rs, c5b_ss, c5b_rs, c6_ss, c6_rs, *halves,
):
    toks, dl = hid.shape
    prompts = members.shape[1]
    tiles = -(-models // 16)
    levels = len(halves) // 2
    half, half_recv = halves[:levels], halves[levels:]
    dp = lax.axis_index("dp")
    f = lax.axis_index("fsdp")
    xy, zh = dp // ZH, dp % ZH
    y, x = xy // X, xy % X
    zl, c = f // NC, f % NC
    base = dp * toks

    def fsdp_peer(k):
        return lax.rem(f + k, F)

    def xy_peer(k):
        return lax.rem(y + k // X, Y) * X + lax.rem(x + k % X, X)

    def xy_dev(q):
        return (q * ZH + zh, f)

    zh_dev = (xy * ZH + (1 - zh), f)
    dp_next, dp_prev = lax.rem(dp + 1, DP), lax.rem(dp + DP - 1, DP)

    loads = [
        pltpu.make_async_copy(lens_hbm, lens_v, load_sem.at[0]),
        pltpu.make_async_copy(battles_hbm, bat_v, load_sem.at[1]),
        pltpu.make_async_copy(gain_hbm, gain_v, load_sem.at[2]),
        pltpu.make_async_copy(head_hbm, head_v, load_sem.at[3]),
    ]
    n_blk = toks // blk
    for i in range(n_blk):
        rows = pl.ds(i * blk, blk)
        loads.append(pltpu.make_async_copy(hidden_hbm.at[rows], hid.at[rows], load_sem.at[4 + i]))
    for cp in loads:
        cp.start()

    barrier = pltpu.get_barrier_semaphore()
    partners = [(dp, fsdp_peer(k)) for k in range(1, F)]
    partners += [xy_dev(xy_peer(k)) for k in range(1, XY)]
    partners += [zh_dev]
    partners += [(dp_prev if r >= F // 2 else dp_next, r) for r in range(F)]
    for dev in partners:
        pl.semaphore_signal(barrier, inc=1, device_id=dev, device_id_type=MESH)

    loads[0].wait()
    lens = jnp.broadcast_to(lens_v[...], (8, prompts))
    len_hi = lens // 32
    len_lo = lens - len_hi * 32
    upto = (
        lax.broadcasted_iota(jnp.int32, (prompts, prompts), 0)
        <= lax.broadcasted_iota(jnp.int32, (prompts, prompts), 1)
    ).astype(F32).astype(BF16)
    ends = (32.0 * nn(len_hi.astype(F32).astype(BF16), upto) + nn(len_lo.astype(F32).astype(BF16), upto))[:1]
    ends = ends.astype(jnp.int32)
    lens = lens[:1]
    starts = ends - lens
    lens_f = lens.astype(F32)
    at_prev = ((starts < base) & (ends > base)).astype(F32)
    at_next = ((starts < base + toks) & (ends > base + toks)).astype(F32)
    owned = ((ends > base) & (ends <= base + toks)).astype(F32)
    before_end = jnp.sum(at_prev * ends.astype(F32), axis=1, keepdims=True)
    from_start = jnp.sum(at_next * starts.astype(F32), axis=1, keepdims=True)
    from_start = jnp.where(jnp.sum(at_next, axis=1, keepdims=True) > 0.0, from_start, 2.0**30)

    loads[2].wait()
    loads[3].wait()
    wide = 16 * tiles
    head_f = head_v[...].astype(F32)
    if wide > models:
        head_f = jnp.concatenate([head_f, jnp.zeros((wide - models, dl), F32)], axis=0)
    wpad[...] = head_f.astype(BF16)
    wp[...] = (head_f * gain_v[...]).astype(BF16)

    def remote(src, dst, ss, rs, dev):
        cp = pltpu.make_async_remote_copy(
            src_ref=src, dst_ref=dst, send_sem=ss, recv_sem=rs, device_id=dev, device_id_type=MESH
        )
        cp.start()
        return cp

    for t in range(tiles, ZL * NC):
        raw16[t // NC, t % NC] = jnp.zeros((16, toks), BF16)
    for i in range(n_blk):
        loads[4 + i].wait()
        rows = pl.ds(i * blk, blk)
        block = nt(wp[...], hid[rows, :])
        raw[:, rows] = block
        for t in range(tiles):
            raw16[t // NC, t % NC, :, rows] = block[16 * t : 16 * t + 16].astype(BF16)

    pl.semaphore_wait(barrier, len(partners))
    c1 = remote(raw16.at[:, 1 - c], c1_recv, c1_ss, c1_rs, (dp, zl * NC + (1 - c)))

    ones_l = jnp.ones((8, LANES), BF16)
    for i in range(n_blk):
        hf = hid[pl.ds(i * blk, blk), :].astype(F32)
        sq = hf * hf
        part = sq[:, :LANES]
        for j in range(1, dl // LANES):
            part = part + sq[:, j * LANES : (j + 1) * LANES]
        part_hi = part.astype(BF16)
        part_lo = (part - part_hi.astype(F32)).astype(BF16)
        sumsq = nt(ones_l, part_hi) + nt(ones_l, part_lo)
        for b in range(blk // LANES):
            q_send[i * (blk // LANES) + b] = sumsq[0:1, b * LANES : (b + 1) * LANES]
    q_cp = [
        remote(q_send.at[fsdp_peer(k)], q_recv.at[k], q_ss.at[k], q_rs.at[k], (dp, fsdp_peer(k)))
        for k in range(1, F)
    ]

    bits = [(zl >> n) % 2 for n in range(levels)]

    def halve(n):
        step = 1 << n
        peer = (zl + step - 2 * step * bits[n]) * NC + c
        return remote(half[n].at[:, 1 - bits[n]], half_recv[n], c2_ss.at[n], c2_rs.at[n], (dp, peer))

    def fold(n):
        for j in range(half_recv[n].shape[0]):
            total = half[n][j, bits[n]].astype(F32) + half_recv[n][j].astype(F32)
            half[n + 1][j // 2, j % 2] = total.astype(BF16)

    c1.wait_recv()
    for k in range(ZL):
        half[0][k // 2, k % 2] = (raw16[k, c].astype(F32) + c1_recv[k].astype(F32)).astype(BF16)
    c2 = [halve(0)]

    for i in range(n_blk):
        pos = base + i * blk + lax.broadcasted_iota(jnp.int32, (blk, prompts), 0)
        inside = (pos >= starts) & (pos < ends)
        members[pl.ds(i * blk, blk), :] = inside.astype(F32).astype(BF16)
    loads[1].wait()
    n_bat = bat_v.shape[1]
    bat_row = lax.broadcasted_iota(jnp.int32, (2 * PAIRS, n_bat), 0)
    bat_lane = lax.broadcasted_iota(jnp.int32, (2 * PAIRS, n_bat), 1)
    bat = jnp.where(bat_row < PAIRS, bat_v[0:1, :], bat_v[1:2, :])
    bat = jnp.where(bat_lane % PAIRS == bat_row % PAIRS, bat, 0)
    judged = lax.broadcasted_iota(jnp.int32, (n_bat, prompts), 0) // PAIRS
    judged = judged == lax.broadcasted_iota(jnp.int32, (n_bat, prompts), 1)
    bat = nn(bat.astype(F32).astype(BF16), judged.astype(F32).astype(BF16))
    ids[...] = nt(bat.astype(BF16), members[...])

    model_of = lax.broadcasted_iota(jnp.int32, (wide, LANES), 0).astype(F32)
    for b in range(toks // LANES):
        lanes = slice(b * LANES, (b + 1) * LANES)
        block = raw[:, lanes]
        id_blk = ids[:, lanes]
        picked = [
            jnp.sum(jnp.where(model_of == id_blk[j : j + 1], block, 0.0), axis=0, keepdims=True)
            for j in range(2 * PAIRS)
        ]
        s1_send[b] = jnp.concatenate(picked, axis=0)

    s1 = [
        remote(s1_send.at[fsdp_peer(k)], s1_recv.at[k], s1_ss.at[k], s1_rs.at[k], (dp, fsdp_peer(k)))
        for k in range(1, F)
    ]
    for cp in q_cp:
        cp.wait_recv()
    acc = q_send[f]
    for k in range(1, F):
        acc = acc + q_recv[k]
    inv_own = lax.rsqrt(acc / width + EPS)
    i_buf[f] = inv_own
    i_cp = [
        remote(i_buf.at[f], i_buf.at[f], i_ss.at[k], i_rs.at[k], (dp, fsdp_peer(k)))
        for k in range(1, F)
    ]

    for cp in s1:
        cp.wait_recv()
    acc = s1_send[f]
    for k in range(1, F):
        acc = acc + s1_recv[k]
    own = acc * inv_own
    s2_buf[f] = own
    s2 = [
        remote(s2_buf.at[f], s2_buf.at[f], s2_ss.at[k], s2_rs.at[k], (dp, fsdp_peer(k)))
        for k in range(1, F)
    ]
    late = f >= F // 2
    pos = base + f * LANES + lax.broadcasted_iota(jnp.int32, (8, LANES), 1)
    pos = pos.astype(F32)
    crossing = jnp.where(late, (pos >= from_start).astype(F32), (pos < before_end).astype(F32))
    column = jnp.sum(jnp.exp(own) * crossing, axis=1, keepdims=True)
    eye = lax.broadcasted_iota(jnp.int32, (8, LANES), 0) == lax.broadcasted_iota(jnp.int32, (8, LANES), 1)
    b_send[...] = jnp.sum(jnp.where(eye, column, 0.0), axis=0, keepdims=True)
    to_dp = jnp.where(late, dp_next, dp_prev)
    b_cp = [
        remote(b_send, b_recv.at[f], b_ss.at[k], b_rs.at[f], (to_dp, lax.rem(f + k, F)))
        for k in range(F)
    ]

    def b_arrival(r):
        return pltpu.make_async_remote_copy(
            src_ref=b_send, dst_ref=b_recv.at[r], send_sem=b_ss.at[r], recv_sem=b_rs.at[r],
            device_id=(to_dp, f), device_id_type=MESH,
        )

    c2[0].wait_recv()
    fold(0)
    c2.append(halve(1))

    for cp in i_cp + s2:
        cp.wait_recv()
    logits = jnp.concatenate([s2_buf[r] for r in range(F)], axis=1)
    inv = jnp.concatenate([i_buf[r] for r in range(F)], axis=1)
    exps = jnp.exp(logits)
    pooled = join3(nn(split3(exps), members[...]))
    for r in range(F):
        b_arrival(r).wait_recv()

    def column_of(rs):
        row = b_recv[rs[0]]
        for r in rs[1:]:
            row = row + b_recv[r]
        return jnp.sum(jnp.where(eye, row, 0.0), axis=1, keepdims=True)

    from_prev = column_of(range(F // 2, F))
    from_next = column_of(range(F // 2))
    pooled = pooled + from_prev * at_prev + from_next * at_next
    pooled = jnp.where(pooled > 0.0, pooled, 1.0)
    for n in range(1, levels - 1):
        c2[n].wait_recv()
        fold(n)
        c2.append(halve(n + 1))
    coef = jnp.log(pooled / lens_f)
    other = jnp.concatenate([coef[PAIRS:], coef[:PAIRS]], axis=0)
    row_of = lax.broadcasted_iota(jnp.int32, (8, prompts), 0)
    sign = jnp.where(row_of < PAIRS, -1.0, 1.0)
    margin = sign * (coef - other)
    softplus = jnp.maximum(margin, 0.0) + jnp.log1p(jnp.exp(-jnp.abs(margin)))
    loss_part = jnp.sum(jnp.where(row_of < PAIRS, softplus * owned, 0.0)) / n_battles
    ratio = sign * (1.0 / (1.0 + jnp.exp(-margin))) / n_battles / pooled
    grads = exps * join3(nt(split3(ratio), members[...]))
    slope = jnp.sum(grads * logits, axis=0, keepdims=True) * inv * inv / width
    grads = grads * inv

    for b in range(toks // LANES):
        lanes = slice(b * LANES, (b + 1) * LANES)
        id_blk = ids[:, lanes]
        full = jnp.zeros((wide, LANES), F32)
        for j in range(2 * PAIRS):
            full = full + jnp.where(model_of == id_blk[j : j + 1], grads[j : j + 1, lanes], 0.0)
        g_t[:, lanes] = full.astype(BF16)
    head_part = nn(g_t[...], hid[...])
    for t in range(tiles):
        g_tile[t] = head_part[16 * t : 16 * t + 16]
        g_send[t] = head_part[16 * t : 16 * t + 16].astype(BF16)
    for t in range(tiles, XY):
        g_tile[t] = jnp.zeros((16, dl), F32)
        g_send[t] = jnp.zeros((16, dl), BF16)
    s4 = [
        remote(g_send.at[xy_peer(k)], s4_recv.at[k], s4_ss.at[k], s4_rs.at[k], xy_dev(xy_peer(k)))
        for k in range(1, XY)
    ]

    c_rows = lax.broadcasted_iota(jnp.int32, (16, toks), 0)
    slope_hi = slope.astype(BF16).astype(F32)
    slope_lo = slope - slope_hi
    slope3 = jnp.where(c_rows == 0, slope_hi, jnp.where(c_rows == 1, slope_lo, 0.0)).astype(BF16)
    ones_w = jnp.ones((16, dl), BF16)
    outs = []
    for i in range(n_blk):
        rows = pl.ds(i * blk, blk)
        gn = tn(g_t[:, rows], wpad[...])
        cb = tn(slope3[:, i * blk : (i + 1) * blk], ones_w)
        out_v[rows, :] = (gain_v[...] * gn - hid[rows, :].astype(F32) * cb).astype(BF16)
        cp = pltpu.make_async_copy(out_v.at[rows], gh_hbm.at[rows], out_sem.at[i])
        cp.start()
        outs.append(cp)

    c2[-1].wait_recv()
    tile = half[-1][0, bits[-1]].astype(F32) + half_recv[-1][0].astype(F32)
    c_blk = join3(nn(split3(jnp.exp(tile * inv)), members[...]))
    mine = jnp.where(f == tiles, loss_part, c_blk)
    c5_all[xy] = mine
    c5 = [
        remote(c5_all.at[xy], c5_all.at[xy], c5_ss.at[k], c5_rs.at[k], xy_dev(xy_peer(k)))
        for k in range(1, XY)
    ]

    for cp in s4:
        cp.wait_recv()
    total = g_tile[xy]
    for k in range(1, XY):
        total = total + s4_recv[k].astype(F32)
    s5_send[...] = total
    s5 = remote(s5_send, s5_recv, s5_ss, s5_rs, zh_dev)

    for cp in c5:
        cp.wait_recv()
    csum = c5_all[0]
    for q in range(1, XY):
        csum = csum + c5_all[q]
    c5_sum[...] = csum
    c5b = remote(c5_sum, c5_other, c5b_ss, c5b_rs, zh_dev)

    s5.wait_recv()
    ag[xy] = (s5_send[...] + s5_recv[...]).astype(BF16)
    s6 = [
        remote(ag.at[xy], ag.at[xy], s6_ss.at[k], s6_rs.at[k], xy_dev(xy_peer(k)))
        for k in range(1, XY)
    ]

    c5b.wait_recv()
    csum = c5_sum[...] + c5_other[...]
    loss_hi = csum.astype(BF16).astype(F32)
    crow = lax.broadcasted_iota(jnp.int32, (16, prompts), 0)
    loss_blk = jnp.where(crow == 0, loss_hi, jnp.where(crow == 1, csum - loss_hi, 0.0))
    coef_blk = jnp.log(csum / lens_f)
    ctab[f] = jnp.where(f == tiles, loss_blk, coef_blk).astype(BF16)
    c6 = [
        remote(ctab.at[f], ctab.at[f], c6_ss.at[k], c6_rs.at[k], (dp, fsdp_peer(k)))
        for k in range(1, F)
    ]

    for cp in s6:
        cp.wait_recv()
    whole = jnp.concatenate([ag[t].astype(F32) for t in range(tiles)], axis=0)
    ghead_ref[...] = (gain_v[...] * whole)[:models]
    ggain_ref[...] = jnp.sum(wpad[...].astype(F32) * whole, axis=0, keepdims=True)

    for cp in c6:
        cp.wait_recv()
    table = jnp.concatenate([ctab[t].astype(F32) for t in range(tiles)], axis=0)
    coef_ref[...] = table[:models]
    loss_ref[0, 0] = jnp.sum(ctab[tiles].astype(F32)[0:2, 0:1])

    for cp in q_cp + i_cp + s1 + s2 + b_cp + s4 + [s5] + s6 + [c1] + c2 + c5 + [c5b] + c6:
        cp.wait_send()
    for cp in outs:
        cp.wait()


def hand_out(
    loss, coef, gh, ghead, ggain, loss_o, coef_o, gh_o, ghead_o, ggain_o,
    coef_v, gh_v, ghead_v, ggain_v, sem_in, sem_out,
):
    rows = gh.shape[0] // 8
    trips = [tuple([r.at[pl.ds(n * rows, rows)] for r in (gh, gh_v, gh_o)]) for n in range(8)]
    trips += [(ghead, ghead_v, ghead_o), (coef, coef_v, coef_o), (ggain, ggain_v, ggain_o)]
    ins, outs = [], []
    for n, (src, mid, dst) in enumerate(trips):
        ins.append(pltpu.make_async_copy(src, mid, sem_in.at[n]))
        outs.append(pltpu.make_async_copy(mid, dst, sem_out.at[n]))
    for cp in ins:
        cp.start()
    loss_o[0, 0] = loss[0, 0]
    for cp_in, cp_out in zip(ins, outs):
        cp_in.wait()
        cp_out.start()
    for cp in outs:
        cp.wait()


def on_device(hidden, gain, head_weight, lengths, battles):
    toks, dl = hidden.shape
    models = head_weight.shape[0]
    prompts = lengths.shape[0]
    n_battles = battles.shape[0]
    tiles = -(-models // 16)
    wide = 16 * tiles
    blk = min(512, toks)
    levels = ZL.bit_length() - 1
    sem = pltpu.SemaphoreType.DMA
    vmem = pl.BlockSpec(memory_space=pltpu.VMEM)
    smem = pl.BlockSpec(memory_space=pltpu.SMEM)
    hbm = pl.BlockSpec(memory_space=pl.ANY)
    V = pltpu.VMEM
    shapes = (
        jax.ShapeDtypeStruct((1, 1), F32),
        jax.ShapeDtypeStruct((models, prompts), F32),
        jax.ShapeDtypeStruct((toks, dl), BF16),
        jax.ShapeDtypeStruct((models, dl), F32),
        jax.ShapeDtypeStruct((1, dl), F32),
    )
    results = pl.pallas_call(
        functools.partial(kernel, models, float(dl * F), float(n_battles), blk),
        out_shape=shapes,
        in_specs=[hbm] * 5,
        out_specs=(smem, vmem, hbm, vmem, vmem),
        scratch_shapes=[
            V((toks, dl), BF16), V((1, dl), F32), V((models, dl), BF16),
            V((1, prompts), jnp.int32), V((2, n_battles), jnp.int32),
            V((wide, dl), BF16), V((wide, dl), BF16),
            V((toks, prompts), BF16), V((2 * PAIRS, toks), F32), V((wide, toks), F32),
            V((ZL, NC, 16, toks), BF16), V((toks, dl), BF16),
            V((F, 1, LANES), F32), V((F, 1, LANES), F32), V((F, 1, LANES), F32),
            V((F, 8, LANES), F32), V((F, 8, LANES), F32), V((F, 8, LANES), F32),
            V((1, LANES), F32), V((F, 1, LANES), F32),
            V((wide, toks), BF16), V((XY, 16, dl), F32), V((XY, 16, dl), BF16),
            V((XY, 16, dl), BF16), V((16, dl), F32), V((16, dl), F32), V((XY, 16, dl), BF16),
            V((ZL, 16, toks), BF16),
            V((XY, 16, prompts), F32), V((16, prompts), F32), V((16, prompts), F32),
            V((F, 16, prompts), BF16),
            sem((4 + toks // blk,)), sem((toks // blk,)),
            sem((F,)), sem((F,)), sem((F,)), sem((F,)),
            sem((F,)), sem((F,)), sem((F,)), sem((F,)), sem((F,)), sem((F,)),
            sem((XY,)), sem((XY,)), sem, sem, sem((XY,)), sem((XY,)),
            sem, sem, sem((levels,)), sem((levels,)), sem((XY,)), sem((XY,)), sem, sem,
            sem((F,)), sem((F,)),
        ]
        + [V((ZL >> (n + 1), 2, 16, toks), BF16) for n in range(levels)]
        + [V((ZL >> (n + 1), 16, toks), BF16) for n in range(levels)],
        compiler_params=pltpu.CompilerParams(
            collective_id=0, has_side_effects=True, vmem_limit_bytes=60 * 2**20
        ),
        name="head",
    )(hidden, gain.reshape(1, dl), head_weight, lengths.reshape(1, prompts), battles.T)
    loss, coef, gh, ghead, ggain = pl.pallas_call(
        hand_out,
        out_shape=shapes,
        in_specs=[smem] + [hbm] * 4,
        out_specs=(smem,) + (hbm,) * 4,
        scratch_shapes=[
            V((models, prompts), F32), V((toks, dl), BF16), V((models, dl), F32), V((1, dl), F32),
            sem((11,)), sem((11,)),
        ],
        compiler_params=pltpu.CompilerParams(vmem_limit_bytes=60 * 2**20),
        name="hand_out",
    )(*results)
    return loss.reshape(()), coef.T, gh, ghead, ggain.reshape(dl)


def solution(mesh):
    placed = (P("dp", "fsdp"), P("fsdp"), P(None, "fsdp"), P(), P())
    return jax.shard_map(
        on_device,
        mesh=mesh,
        in_specs=placed,
        out_specs=(P(), P(), P("dp", "fsdp"), P(None, "fsdp"), P("fsdp")),
        check_vma=False,
    )
```

```python
import functools

import jax
import jax.numpy as jnp
from jax import lax
from jax.experimental import pallas as pl
from jax.experimental.pallas import tpu as pltpu
from jax.sharding import PartitionSpec as P

Y, X, ZH, ZL, NC = 4, 4, 2, 8, 2
XY, F, DP = Y * X, ZL * NC, Y * X * ZH
LANES = 128
PAIRS = 4
EPS = 1e-06
MESH = pl.DeviceIdType.MESH
F32, BF16 = jnp.float32, jnp.bfloat16


def nn(a, b):
    return lax.dot_general(a, b, (((1,), (0,)), ((), ())), preferred_element_type=F32)


def nt(a, b):
    return lax.dot_general(a, b, (((1,), (1,)), ((), ())), preferred_element_type=F32)


def tn(a, b):
    return lax.dot_general(a, b, (((0,), (0,)), ((), ())), preferred_element_type=F32)


def split3(x):
    hi = x.astype(BF16).astype(F32)
    mid = (x - hi).astype(BF16).astype(F32)
    return jnp.concatenate([hi, mid, x - hi - mid], axis=0).astype(BF16)


def join3(x):
    rows = x.shape[0] // 3
    return x[:rows] + x[rows : 2 * rows] + x[2 * rows :]


def kernel(
    models, width, n_battles, blk,
    hidden_hbm, gain_hbm, head_hbm, lens_hbm, battles_hbm,
    loss_out, coef_out, gh_out, ghead_out, ggain_out,
    hid, gain_v, head_v, lens_v, bat_v, wp, wpad, members, ids, raw, raw16, out_v,
    loss_v, coef_v, ghead_v, ggain_v,
    q_send, q_recv, i_buf, s1_send, s1_recv, s2_buf, b_send, b_recv, g_t, g_tile, g_send, s4_recv,
    s5_send, s5_recv, ag, c1_recv, c5_all, c5_sum, c5_other, ctab,
    load_sem, out_sem, q_ss, q_rs, i_ss, i_rs, s1_ss, s1_rs, s2_ss, s2_rs, b_ss, b_rs, s4_ss, s4_rs,
    s5_ss, s5_rs, s6_ss, s6_rs, c1_ss, c1_rs, c2_ss, c2_rs, c5_ss, c5_rs, c5b_ss, c5b_rs, c6_ss, c6_rs, *halves,
):
    toks, dl = hid.shape
    prompts = members.shape[1]
    tiles = -(-models // 16)
    levels = len(halves) // 2
    half, half_recv = halves[:levels], halves[levels:]
    dp = lax.axis_index("dp")
    f = lax.axis_index("fsdp")
    xy, zh = dp // ZH, dp % ZH
    y, x = xy // X, xy % X
    zl, c = f // NC, f % NC
    base = dp * toks

    def fsdp_peer(k):
        return lax.rem(f + k, F)

    def xy_peer(k):
        return lax.rem(y + k // X, Y) * X + lax.rem(x + k % X, X)

    def xy_dev(q):
        return (q * ZH + zh, f)

    zh_dev = (xy * ZH + (1 - zh), f)
    dp_next, dp_prev = lax.rem(dp + 1, DP), lax.rem(dp + DP - 1, DP)

    loads = [
        pltpu.make_async_copy(lens_hbm, lens_v, load_sem.at[0]),
        pltpu.make_async_copy(battles_hbm, bat_v, load_sem.at[1]),
        pltpu.make_async_copy(gain_hbm, gain_v, load_sem.at[2]),
        pltpu.make_async_copy(head_hbm, head_v, load_sem.at[3]),
    ]
    n_blk = toks // blk
    for i in range(n_blk):
        rows = pl.ds(i * blk, blk)
        loads.append(pltpu.make_async_copy(hidden_hbm.at[rows], hid.at[rows], load_sem.at[4 + i]))
    for cp in loads:
        cp.start()

    barrier = pltpu.get_barrier_semaphore()
    partners = [(dp, fsdp_peer(k)) for k in range(1, F)]
    partners += [xy_dev(xy_peer(k)) for k in range(1, XY)]
    partners += [zh_dev]
    partners += [(dp_prev if r >= F // 2 else dp_next, r) for r in range(F)]
    for dev in partners:
        pl.semaphore_signal(barrier, inc=1, device_id=dev, device_id_type=MESH)

    loads[0].wait()
    lens = jnp.broadcast_to(lens_v[...], (8, prompts))
    len_hi = lens // 32
    len_lo = lens - len_hi * 32
    upto = (
        lax.broadcasted_iota(jnp.int32, (prompts, prompts), 0)
        <= lax.broadcasted_iota(jnp.int32, (prompts, prompts), 1)
    ).astype(F32).astype(BF16)
    ends = (32.0 * nn(len_hi.astype(F32).astype(BF16), upto) + nn(len_lo.astype(F32).astype(BF16), upto))[:1]
    ends = ends.astype(jnp.int32)
    lens = lens[:1]
    starts = ends - lens
    lens_f = lens.astype(F32)
    at_prev = ((starts < base) & (ends > base)).astype(F32)
    at_next = ((starts < base + toks) & (ends > base + toks)).astype(F32)
    owned = ((ends > base) & (ends <= base + toks)).astype(F32)
    before_end = jnp.sum(at_prev * ends.astype(F32), axis=1, keepdims=True)
    from_start = jnp.sum(at_next * starts.astype(F32), axis=1, keepdims=True)
    from_start = jnp.where(jnp.sum(at_next, axis=1, keepdims=True) > 0.0, from_start, 2.0**30)

    loads[2].wait()
    loads[3].wait()
    wide = 16 * tiles
    head_f = head_v[...].astype(F32)
    if wide > models:
        head_f = jnp.concatenate([head_f, jnp.zeros((wide - models, dl), F32)], axis=0)
    wpad[...] = head_f.astype(BF16)
    wp[...] = (head_f * gain_v[...]).astype(BF16)

    def remote(src, dst, ss, rs, dev):
        cp = pltpu.make_async_remote_copy(
            src_ref=src, dst_ref=dst, send_sem=ss, recv_sem=rs, device_id=dev, device_id_type=MESH
        )
        cp.start()
        return cp

    def scatter(src, dst, ss, rs, peer, dev):
        for k in range(1, dst.shape[0]):
            remote(src.at[peer(k)], dst.at[k], ss, rs, dev(peer(k)))
        rest = dst.at[pl.ds(1, dst.shape[0] - 1)]
        return pltpu.make_async_remote_copy(
            src_ref=rest, dst_ref=rest, send_sem=ss, recv_sem=rs, device_id=dev(peer(1)), device_id_type=MESH
        )

    def gather(buf, ss, rs, peer, dev):
        for k in range(1, buf.shape[0]):
            remote(buf.at[0], buf.at[k], ss, rs, dev(peer(k)))
        rest = buf.at[pl.ds(1, buf.shape[0] - 1)]
        return pltpu.make_async_remote_copy(
            src_ref=rest, dst_ref=rest, send_sem=ss, recv_sem=rs, device_id=dev(peer(1)), device_id_type=MESH
        )

    def fsdp_dev(r):
        return (dp, r)

    def fsdp_slot(r):
        return lax.rem(f + F - r, F)

    def xy_slot(q):
        return lax.rem(y + Y - q // X, Y) * X + lax.rem(x + X - q % X, X)

    ones_l = jnp.ones((8, LANES), BF16)
    for i in range(n_blk):
        loads[4 + i].wait()
        hf = hid[pl.ds(i * blk, blk), :].astype(F32)
        sq = hf * hf
        part = sq[:, :LANES]
        for j in range(1, dl // LANES):
            part = part + sq[:, j * LANES : (j + 1) * LANES]
        part_hi = part.astype(BF16)
        part_lo = (part - part_hi.astype(F32)).astype(BF16)
        sumsq = nt(ones_l, part_hi) + nt(ones_l, part_lo)
        for b in range(blk // LANES):
            q_send[i * (blk // LANES) + b] = sumsq[0:1, b * LANES : (b + 1) * LANES]
    pl.semaphore_wait(barrier, len(partners))
    q_cp = scatter(q_send, q_recv, q_ss, q_rs, fsdp_peer, fsdp_dev)

    for t in range(tiles, ZL * NC):
        raw16[t // NC, t % NC] = jnp.zeros((16, toks), BF16)
    for i in range(n_blk):
        rows = pl.ds(i * blk, blk)
        block = nt(wp[...], hid[rows, :])
        raw[:, rows] = block
        for t in range(tiles):
            raw16[t // NC, t % NC, :, rows] = block[16 * t : 16 * t + 16].astype(BF16)

    c1 = remote(raw16.at[:, 1 - c], c1_recv, c1_ss, c1_rs, (dp, zl * NC + (1 - c)))

    bits = [(zl >> n) % 2 for n in range(levels)]

    def halve(n):
        step = 1 << n
        peer = (zl + step - 2 * step * bits[n]) * NC + c
        return remote(half[n].at[:, 1 - bits[n]], half_recv[n], c2_ss.at[n], c2_rs.at[n], (dp, peer))

    def fold(n):
        for j in range(half_recv[n].shape[0]):
            total = half[n][j, bits[n]].astype(F32) + half_recv[n][j].astype(F32)
            half[n + 1][j // 2, j % 2] = total.astype(BF16)

    for i in range(n_blk):
        pos = base + i * blk + lax.broadcasted_iota(jnp.int32, (blk, prompts), 0)
        inside = (pos >= starts) & (pos < ends)
        members[pl.ds(i * blk, blk), :] = inside.astype(F32).astype(BF16)
    loads[1].wait()
    n_bat = bat_v.shape[1]
    bat_row = lax.broadcasted_iota(jnp.int32, (2 * PAIRS, n_bat), 0)
    bat_lane = lax.broadcasted_iota(jnp.int32, (2 * PAIRS, n_bat), 1)
    bat = jnp.where(bat_row < PAIRS, bat_v[0:1, :], bat_v[1:2, :])
    bat = jnp.where(bat_lane % PAIRS == bat_row % PAIRS, bat, 0)
    judged = lax.broadcasted_iota(jnp.int32, (n_bat, prompts), 0) // PAIRS
    judged = judged == lax.broadcasted_iota(jnp.int32, (n_bat, prompts), 1)
    bat = nn(bat.astype(F32).astype(BF16), judged.astype(F32).astype(BF16))
    ids[...] = nt(bat.astype(BF16), members[...])

    c1.wait_recv()
    for k in range(ZL):
        half[0][k // 2, k % 2] = (raw16[k, c].astype(F32) + c1_recv[k].astype(F32)).astype(BF16)
    c2 = [halve(0)]

    model_of = lax.broadcasted_iota(jnp.int32, (wide, LANES), 0).astype(F32)
    for b in range(toks // LANES):
        lanes = slice(b * LANES, (b + 1) * LANES)
        block = raw[:, lanes]
        id_blk = ids[:, lanes]
        picked = [
            jnp.sum(jnp.where(model_of == id_blk[j : j + 1], block, 0.0), axis=0, keepdims=True)
            for j in range(2 * PAIRS)
        ]
        s1_send[b] = jnp.concatenate(picked, axis=0)

    s1 = scatter(s1_send, s1_recv, s1_ss, s1_rs, fsdp_peer, fsdp_dev)

    q_cp.wait_recv()
    acc = q_send[f]
    for k in range(1, F):
        acc = acc + q_recv[k]
    inv_own = lax.rsqrt(acc / width + EPS)
    i_buf[0] = inv_own
    i_cp = gather(i_buf, i_ss, i_rs, fsdp_peer, fsdp_dev)

    s1.wait_recv()
    acc = s1_send[f]
    for k in range(1, F):
        acc = acc + s1_recv[k]
    own = acc * inv_own
    s2_buf[0] = own
    s2 = gather(s2_buf, s2_ss, s2_rs, fsdp_peer, fsdp_dev)
    late = f >= F // 2
    pos = base + f * LANES + lax.broadcasted_iota(jnp.int32, (8, LANES), 1)
    pos = pos.astype(F32)
    crossing = jnp.where(late, (pos >= from_start).astype(F32), (pos < before_end).astype(F32))
    column = jnp.sum(jnp.exp(own) * crossing, axis=1, keepdims=True)
    eye = lax.broadcasted_iota(jnp.int32, (8, LANES), 0) == lax.broadcasted_iota(jnp.int32, (8, LANES), 1)
    b_send[...] = jnp.sum(jnp.where(eye, column, 0.0), axis=0, keepdims=True)
    to_dp = jnp.where(late, dp_next, dp_prev)
    for k in range(F):
        remote(b_send, b_recv.at[f], b_ss, b_rs, (to_dp, lax.rem(f + k, F)))
    b_cp = pltpu.make_async_remote_copy(
        src_ref=b_recv, dst_ref=b_recv, send_sem=b_ss, recv_sem=b_rs,
        device_id=(to_dp, f), device_id_type=MESH,
    )

    c2[0].wait_recv()
    fold(0)
    c2.append(halve(1))

    for n in range(1, levels - 1):
        c2[n].wait_recv()
        fold(n)
        c2.append(halve(n + 1))

    i_cp.wait_recv()
    inv = jnp.concatenate([i_buf[fsdp_slot(r)] for r in range(F)], axis=1)
    s2.wait_recv()
    logits = jnp.concatenate([s2_buf[fsdp_slot(r)] for r in range(F)], axis=1)
    exps = jnp.exp(logits)
    pooled = join3(nn(split3(exps), members[...]))
    b_cp.wait_recv()

    def column_of(rs):
        row = b_recv[rs[0]]
        for r in rs[1:]:
            row = row + b_recv[r]
        return jnp.sum(jnp.where(eye, row, 0.0), axis=1, keepdims=True)

    from_prev = column_of(range(F // 2, F))
    from_next = column_of(range(F // 2))
    pooled = pooled + from_prev * at_prev + from_next * at_next
    pooled = jnp.where(pooled > 0.0, pooled, 1.0)
    coef = jnp.log(pooled / lens_f)
    other = jnp.concatenate([coef[PAIRS:], coef[:PAIRS]], axis=0)
    row_of = lax.broadcasted_iota(jnp.int32, (8, prompts), 0)
    sign = jnp.where(row_of < PAIRS, -1.0, 1.0)
    margin = sign * (coef - other)
    softplus = jnp.maximum(margin, 0.0) + jnp.log1p(jnp.exp(-jnp.abs(margin)))
    loss_part = jnp.sum(jnp.where(row_of < PAIRS, softplus * owned, 0.0)) / n_battles
    ratio = sign * (1.0 / (1.0 + jnp.exp(-margin))) / n_battles / pooled
    grads = exps * join3(nt(split3(ratio), members[...]))
    slope = jnp.sum(grads * logits, axis=0, keepdims=True) * inv * inv / width
    grads = grads * inv

    for b in range(toks // LANES):
        lanes = slice(b * LANES, (b + 1) * LANES)
        id_blk = ids[:, lanes]
        full = jnp.zeros((wide, LANES), F32)
        for j in range(2 * PAIRS):
            full = full + jnp.where(model_of == id_blk[j : j + 1], grads[j : j + 1, lanes], 0.0)
        g_t[:, lanes] = full.astype(BF16)
    head_part = nn(g_t[...], hid[...])
    for t in range(tiles):
        g_tile[t] = head_part[16 * t : 16 * t + 16]
        g_send[t] = head_part[16 * t : 16 * t + 16].astype(BF16)
    for t in range(tiles, XY):
        g_tile[t] = jnp.zeros((16, dl), F32)
        g_send[t] = jnp.zeros((16, dl), BF16)
    s4 = scatter(g_send, s4_recv, s4_ss, s4_rs, xy_peer, xy_dev)

    c2[-1].wait_recv()
    tile = half[-1][0, bits[-1]].astype(F32) + half_recv[-1][0].astype(F32)
    c_blk = join3(nn(split3(jnp.exp(tile * inv)), members[...]))
    mine = jnp.where(f == tiles, loss_part, c_blk)
    c5_all[0] = mine
    c5 = gather(c5_all, c5_ss, c5_rs, xy_peer, xy_dev)

    c_rows = lax.broadcasted_iota(jnp.int32, (16, toks), 0)
    slope_hi = slope.astype(BF16).astype(F32)
    slope_lo = slope - slope_hi
    slope3 = jnp.where(c_rows == 0, slope_hi, jnp.where(c_rows == 1, slope_lo, 0.0)).astype(BF16)
    ones_w = jnp.ones((16, dl), BF16)
    outs = []
    for i in range(n_blk):
        rows = pl.ds(i * blk, blk)
        gn = tn(g_t[:, rows], wpad[...])
        cb = tn(slope3[:, i * blk : (i + 1) * blk], ones_w)
        out_v[rows, :] = (gain_v[...] * gn - hid[rows, :].astype(F32) * cb).astype(BF16)
        cp = pltpu.make_async_copy(out_v.at[rows], gh_out.at[rows], out_sem.at[i])
        cp.start()
        outs.append(cp)

    s4.wait_recv()
    total = g_tile[xy]
    for k in range(1, XY):
        total = total + s4_recv[k].astype(F32)
    s5_send[...] = total
    s5 = remote(s5_send, s5_recv, s5_ss, s5_rs, zh_dev)

    c5.wait_recv()
    csum = c5_all[xy_slot(0)]
    for q in range(1, XY):
        csum = csum + c5_all[xy_slot(q)]
    c5_sum[...] = csum
    c5b = remote(c5_sum, c5_other, c5b_ss, c5b_rs, zh_dev)

    s5.wait_recv()
    ag[0] = (s5_send[...] + s5_recv[...]).astype(BF16)
    s6 = gather(ag, s6_ss, s6_rs, xy_peer, xy_dev)

    c5b.wait_recv()
    csum = c5_sum[...] + c5_other[...]
    loss_hi = csum.astype(BF16).astype(F32)
    crow = lax.broadcasted_iota(jnp.int32, (16, prompts), 0)
    loss_blk = jnp.where(crow == 0, loss_hi, jnp.where(crow == 1, csum - loss_hi, 0.0))
    coef_blk = jnp.log(csum / lens_f)
    ctab[0] = jnp.where(f == tiles, loss_blk, coef_blk).astype(BF16)
    c6 = gather(ctab, c6_ss, c6_rs, fsdp_peer, fsdp_dev)

    def hand(n, src, dst):
        cp = pltpu.make_async_copy(src, dst, out_sem.at[n_blk + n])
        cp.start()
        outs.append(cp)

    s6.wait_recv()
    whole = jnp.concatenate([ag[xy_slot(t)].astype(F32) for t in range(tiles)], axis=0)
    ghead_v[...] = (gain_v[...] * whole)[:models]
    ggain_v[...] = jnp.sum(wpad[...].astype(F32) * whole, axis=0, keepdims=True)
    hand(0, ghead_v, ghead_out)
    hand(1, ggain_v, ggain_out)

    c6.wait_recv()
    table = jnp.concatenate([ctab[fsdp_slot(t)].astype(F32) for t in range(tiles)], axis=0)
    coef_v[...] = table[:models]
    loss_v[...] = jnp.sum(ctab[fsdp_slot(tiles)].astype(F32)[0:2, 0:1], axis=0, keepdims=True)
    hand(2, coef_v, coef_out)
    hand(3, loss_v, loss_out)

    for cp in [q_cp, i_cp, s1, s2, b_cp, s4, s5, s6, c1] + c2 + [c5, c5b, c6]:
        cp.wait_send()
    for cp in outs:
        cp.wait()


def hand_out(loss, coef, gh, ghead, ggain, loss_o, coef_o, gh_o, ghead_o, ggain_o, sems):
    rows = gh.shape[0] // 4
    pairs = [(gh.at[pl.ds(n * rows, rows)], gh_o.at[pl.ds(n * rows, rows)]) for n in range(4)]
    pairs += [(ghead, ghead_o), (coef, coef_o), (ggain, ggain_o), (loss, loss_o)]
    cps = [pltpu.make_async_copy(a, b, sems.at[n]) for n, (a, b) in enumerate(pairs)]
    for cp in cps:
        cp.start()
    for cp in cps:
        cp.wait()


def on_device(hidden, gain, head_weight, lengths, battles):
    toks, dl = hidden.shape
    models = head_weight.shape[0]
    prompts = lengths.shape[0]
    n_battles = battles.shape[0]
    tiles = -(-models // 16)
    wide = 16 * tiles
    blk = min(512, toks)
    levels = ZL.bit_length() - 1
    sem = pltpu.SemaphoreType.DMA
    hbm = pl.BlockSpec(memory_space=pl.ANY)
    V = pltpu.VMEM
    kinds = (
        ((1, 1), F32), ((models, prompts), F32), ((toks, dl), BF16), ((models, dl), F32), ((1, dl), F32)
    )
    operands = [hidden, gain.reshape(1, dl), head_weight, lengths.reshape(1, prompts), battles.T]
    operands = [pltpu.with_memory_space_constraint(a, pltpu.HBM) for a in operands]
    results = pl.pallas_call(
        functools.partial(kernel, models, float(dl * F), float(n_battles), blk),
        out_shape=tuple(pltpu.VMEM(*k) for k in kinds),
        in_specs=[hbm] * 5,
        out_specs=(hbm,) * 5,
        scratch_shapes=[
            V((toks, dl), BF16), V((1, dl), F32), V((models, dl), BF16),
            V((1, prompts), jnp.int32), V((2, n_battles), jnp.int32),
            V((wide, dl), BF16), V((wide, dl), BF16),
            V((toks, prompts), BF16), V((2 * PAIRS, toks), F32), V((wide, toks), F32),
            V((ZL, NC, 16, toks), BF16), V((toks, dl), BF16),
            V((1, 1), F32), V((models, prompts), F32), V((models, dl), F32), V((1, dl), F32),
            V((F, 1, LANES), F32), V((F, 1, LANES), F32), V((F, 1, LANES), F32),
            V((F, 8, LANES), F32), V((F, 8, LANES), F32), V((F, 8, LANES), F32),
            V((1, LANES), F32), V((F, 1, LANES), F32),
            V((wide, toks), BF16), V((XY, 16, dl), F32), V((XY, 16, dl), BF16),
            V((XY, 16, dl), BF16), V((16, dl), F32), V((16, dl), F32), V((XY, 16, dl), BF16),
            V((ZL, 16, toks), BF16),
            V((XY, 16, prompts), F32), V((16, prompts), F32), V((16, prompts), F32),
            V((F, 16, prompts), BF16),
            sem((4 + toks // blk,)), sem((4 + toks // blk,)),
            *[sem] * 18, sem((levels,)), sem((levels,)), *[sem] * 6,
        ]
        + [V((ZL >> (n + 1), 2, 16, toks), BF16) for n in range(levels)]
        + [V((ZL >> (n + 1), 16, toks), BF16) for n in range(levels)],
        compiler_params=pltpu.CompilerParams(
            collective_id=0, has_side_effects=True, vmem_limit_bytes=48 * 2**20
        ),
        name="head",
    )(*operands)
    loss, coef, gh, ghead, ggain = pl.pallas_call(
        hand_out,
        out_shape=tuple(pltpu.HBM(*k) for k in kinds),
        in_specs=[hbm] * 5,
        out_specs=(hbm,) * 5,
        scratch_shapes=[sem((8,))],
        name="hand_out",
    )(*results)
    return loss.reshape(()), coef.T, gh, ghead, ggain.reshape(dl)


def solution(mesh):
    placed = (P("dp", "fsdp"), P("fsdp"), P(None, "fsdp"), P(), P())
    return jax.shard_map(
        on_device,
        mesh=mesh,
        in_specs=placed,
        out_specs=(P(), P(), P("dp", "fsdp"), P(None, "fsdp"), P("fsdp")),
        check_vma=False,
    )
```

```python
import functools

import jax
import jax.numpy as jnp
from jax import lax
from jax.experimental import pallas as pl
from jax.experimental.pallas import tpu as pltpu
from jax.sharding import PartitionSpec as P

Y, X, ZH, ZL, NC = 4, 4, 2, 8, 2
XY, F, DP = Y * X, ZL * NC, Y * X * ZH
LANES = 128
PAIRS = 4
EPS = 1e-06
MESH = pl.DeviceIdType.MESH
F32, BF16 = jnp.float32, jnp.bfloat16


def nn(a, b):
    return lax.dot_general(a, b, (((1,), (0,)), ((), ())), preferred_element_type=F32)


def nt(a, b):
    return lax.dot_general(a, b, (((1,), (1,)), ((), ())), preferred_element_type=F32)


def tn(a, b):
    return lax.dot_general(a, b, (((0,), (0,)), ((), ())), preferred_element_type=F32)


def split3(x):
    hi = x.astype(BF16).astype(F32)
    mid = (x - hi).astype(BF16).astype(F32)
    return jnp.concatenate([hi, mid, x - hi - mid], axis=0).astype(BF16)


def join3(x):
    rows = x.shape[0] // 3
    return x[:rows] + x[rows : 2 * rows] + x[2 * rows :]


def kernel(
    models, width, n_battles, blk,
    hidden_hbm, gain_hbm, head_hbm, lens_hbm, battles_hbm,
    loss_out, coef_out, gh_out, ghead_out, ggain_out,
    hid, gain_v, head_v, lens_v, bat_v, wp, wpad, members, ids, raw, raw16, out_v,
    loss_v, coef_v, ghead_v, ggain_v,
    q_send, q_recv, i_buf, s1_send, s1_recv, s2_buf, b_send, b_recv, g_t, g_tile, g_send, s4_recv,
    s5_send, s5_recv, ag, c1_recv, c5_all, c5_sum, c5_other, ctab,
    load_sem, out_sem, q_ss, q_rs, i_ss, i_rs, s1_ss, s1_rs, s2_ss, s2_rs, b_ss, b_rs, s4_ss, s4_rs,
    s5_ss, s5_rs, s6_ss, s6_rs, c1_ss, c1_rs, c2_ss, c2_rs, c5_ss, c5_rs, c5b_ss, c5b_rs, c6_ss, c6_rs, *halves,
):
    toks, dl = hid.shape
    prompts = members.shape[1]
    tiles = -(-models // 16)
    levels = len(halves) // 2
    half, half_recv = halves[:levels], halves[levels:]
    dp = lax.axis_index("dp")
    f = lax.axis_index("fsdp")
    xy, zh = dp // ZH, dp % ZH
    y, x = xy // X, xy % X
    zl, c = f // NC, f % NC
    base = dp * toks

    def fsdp_peer(k):
        return lax.rem(f + k, F)

    def xy_peer(k):
        return lax.rem(y + k // X, Y) * X + lax.rem(x + k % X, X)

    def xy_dev(q):
        return (q * ZH + zh, f)

    zh_dev = (xy * ZH + (1 - zh), f)
    dp_next, dp_prev = lax.rem(dp + 1, DP), lax.rem(dp + DP - 1, DP)

    loads = [
        pltpu.make_async_copy(lens_hbm, lens_v, load_sem.at[0]),
        pltpu.make_async_copy(battles_hbm, bat_v, load_sem.at[1]),
        pltpu.make_async_copy(gain_hbm, gain_v, load_sem.at[2]),
        pltpu.make_async_copy(head_hbm, head_v, load_sem.at[3]),
    ]
    n_blk = toks // blk
    for i in range(n_blk):
        rows = pl.ds(i * blk, blk)
        loads.append(pltpu.make_async_copy(hidden_hbm.at[rows], hid.at[rows], load_sem.at[4 + i]))
    for cp in loads:
        cp.start()

    barrier = pltpu.get_barrier_semaphore()
    partners = [(dp, fsdp_peer(k)) for k in range(1, F)]
    partners += [xy_dev(xy_peer(k)) for k in range(1, XY)]
    partners += [zh_dev]
    partners += [(dp_prev if r >= F // 2 else dp_next, r) for r in range(F)]
    for dev in partners:
        pl.semaphore_signal(barrier, inc=1, device_id=dev, device_id_type=MESH)

    loads[0].wait()
    lens = jnp.broadcast_to(lens_v[...], (8, prompts))
    len_hi = lens // 32
    len_lo = lens - len_hi * 32
    upto = (
        lax.broadcasted_iota(jnp.int32, (prompts, prompts), 0)
        <= lax.broadcasted_iota(jnp.int32, (prompts, prompts), 1)
    ).astype(F32).astype(BF16)
    ends = (32.0 * nn(len_hi.astype(F32).astype(BF16), upto) + nn(len_lo.astype(F32).astype(BF16), upto))[:1]
    ends = ends.astype(jnp.int32)
    lens = lens[:1]
    starts = ends - lens
    lens_f = lens.astype(F32)
    at_prev = ((starts < base) & (ends > base)).astype(F32)
    at_next = ((starts < base + toks) & (ends > base + toks)).astype(F32)
    owned = ((ends > base) & (ends <= base + toks)).astype(F32)
    before_end = jnp.sum(at_prev * ends.astype(F32), axis=1, keepdims=True)
    from_start = jnp.sum(at_next * starts.astype(F32), axis=1, keepdims=True)
    from_start = jnp.where(jnp.sum(at_next, axis=1, keepdims=True) > 0.0, from_start, 2.0**30)

    loads[2].wait()
    loads[3].wait()
    wide = 16 * tiles
    head_f = head_v[...].astype(F32)
    if wide > models:
        head_f = jnp.concatenate([head_f, jnp.zeros((wide - models, dl), F32)], axis=0)
    wpad[...] = head_f.astype(BF16)
    wp[...] = (head_f * gain_v[...]).astype(BF16)

    def remote(src, dst, ss, rs, dev):
        cp = pltpu.make_async_remote_copy(
            src_ref=src, dst_ref=dst, send_sem=ss, recv_sem=rs, device_id=dev, device_id_type=MESH
        )
        cp.start()
        return cp

    def scatter(src, dst, ss, rs, peer, dev):
        for k in range(1, dst.shape[0]):
            remote(src.at[peer(k)], dst.at[k], ss, rs, dev(peer(k)))
        rest = dst.at[pl.ds(1, dst.shape[0] - 1)]
        return pltpu.make_async_remote_copy(
            src_ref=rest, dst_ref=rest, send_sem=ss, recv_sem=rs, device_id=dev(peer(1)), device_id_type=MESH
        )

    def gather(buf, ss, rs, peer, dev):
        for k in range(1, buf.shape[0]):
            remote(buf.at[0], buf.at[k], ss, rs, dev(peer(k)))
        rest = buf.at[pl.ds(1, buf.shape[0] - 1)]
        return pltpu.make_async_remote_copy(
            src_ref=rest, dst_ref=rest, send_sem=ss, recv_sem=rs, device_id=dev(peer(1)), device_id_type=MESH
        )

    def fsdp_dev(r):
        return (dp, r)

    def fsdp_slot(r):
        return lax.rem(f + F - r, F)

    def xy_slot(q):
        return lax.rem(y + Y - q // X, Y) * X + lax.rem(x + X - q % X, X)

    for t in range(tiles, ZL * NC):
        raw16[t // NC, t % NC] = jnp.zeros((16, toks), BF16)
    for i in range(n_blk):
        loads[4 + i].wait()
        rows = pl.ds(i * blk, blk)
        block = nt(wp[...], hid[rows, :])
        raw[:, rows] = block
        for t in range(tiles):
            raw16[t // NC, t % NC, :, rows] = block[16 * t : 16 * t + 16].astype(BF16)

    pl.semaphore_wait(barrier, len(partners))
    c1 = remote(raw16.at[:, 1 - c], c1_recv, c1_ss, c1_rs, (dp, zl * NC + (1 - c)))

    bits = [(zl >> n) % 2 for n in range(levels)]

    def halve(n):
        step = 1 << n
        peer = (zl + step - 2 * step * bits[n]) * NC + c
        return remote(half[n].at[:, 1 - bits[n]], half_recv[n], c2_ss.at[n], c2_rs.at[n], (dp, peer))

    def fold(n):
        for j in range(half_recv[n].shape[0]):
            total = half[n][j, bits[n]].astype(F32) + half_recv[n][j].astype(F32)
            half[n + 1][j // 2, j % 2] = total.astype(BF16)

    for i in range(n_blk):
        pos = base + i * blk + lax.broadcasted_iota(jnp.int32, (blk, prompts), 0)
        inside = (pos >= starts) & (pos < ends)
        members[pl.ds(i * blk, blk), :] = inside.astype(F32).astype(BF16)
    loads[1].wait()
    n_bat = bat_v.shape[1]
    bat_row = lax.broadcasted_iota(jnp.int32, (2 * PAIRS, n_bat), 0)
    bat_lane = lax.broadcasted_iota(jnp.int32, (2 * PAIRS, n_bat), 1)
    bat = jnp.where(bat_row < PAIRS, bat_v[0:1, :], bat_v[1:2, :])
    bat = jnp.where(bat_lane % PAIRS == bat_row % PAIRS, bat, 0)
    judged = lax.broadcasted_iota(jnp.int32, (n_bat, prompts), 0) // PAIRS
    judged = judged == lax.broadcasted_iota(jnp.int32, (n_bat, prompts), 1)
    bat = nn(bat.astype(F32).astype(BF16), judged.astype(F32).astype(BF16))
    ids[...] = nt(bat.astype(BF16), members[...])

    model_of = lax.broadcasted_iota(jnp.int32, (wide, LANES), 0).astype(F32)
    for b in range(toks // LANES):
        lanes = slice(b * LANES, (b + 1) * LANES)
        block = raw[:, lanes]
        id_blk = ids[:, lanes]
        picked = [
            jnp.sum(jnp.where(model_of == id_blk[j : j + 1], block, 0.0), axis=0, keepdims=True)
            for j in range(2 * PAIRS)
        ]
        s1_send[b] = jnp.concatenate(picked, axis=0)

    s1 = scatter(s1_send, s1_recv, s1_ss, s1_rs, fsdp_peer, fsdp_dev)

    ones_l = jnp.ones((8, LANES), BF16)
    for i in range(n_blk):
        hf = hid[pl.ds(i * blk, blk), :].astype(F32)
        sq = hf * hf
        part = sq[:, :LANES]
        for j in range(1, dl // LANES):
            part = part + sq[:, j * LANES : (j + 1) * LANES]
        part_hi = part.astype(BF16)
        part_lo = (part - part_hi.astype(F32)).astype(BF16)
        sumsq = nt(ones_l, part_hi) + nt(ones_l, part_lo)
        for b in range(blk // LANES):
            q_send[i * (blk // LANES) + b] = sumsq[0:1, b * LANES : (b + 1) * LANES]
    q_cp = scatter(q_send, q_recv, q_ss, q_rs, fsdp_peer, fsdp_dev)

    c1.wait_recv()
    for k in range(ZL):
        half[0][k // 2, k % 2] = (raw16[k, c].astype(F32) + c1_recv[k].astype(F32)).astype(BF16)
    c2 = [halve(0)]

    q_cp.wait_recv()
    acc = q_send[f]
    for k in range(1, F):
        acc = acc + q_recv[k]
    inv_own = lax.rsqrt(acc / width + EPS)
    i_buf[0] = inv_own
    i_cp = gather(i_buf, i_ss, i_rs, fsdp_peer, fsdp_dev)

    s1.wait_recv()
    acc = s1_send[f]
    for k in range(1, F):
        acc = acc + s1_recv[k]
    own = acc * inv_own
    s2_buf[0] = own
    s2 = gather(s2_buf, s2_ss, s2_rs, fsdp_peer, fsdp_dev)
    late = f >= F // 2
    pos = base + f * LANES + lax.broadcasted_iota(jnp.int32, (8, LANES), 1)
    pos = pos.astype(F32)
    crossing = jnp.where(late, (pos >= from_start).astype(F32), (pos < before_end).astype(F32))
    column = jnp.sum(jnp.exp(own) * crossing, axis=1, keepdims=True)
    eye = lax.broadcasted_iota(jnp.int32, (8, LANES), 0) == lax.broadcasted_iota(jnp.int32, (8, LANES), 1)
    b_send[...] = jnp.sum(jnp.where(eye, column, 0.0), axis=0, keepdims=True)
    to_dp = jnp.where(late, dp_next, dp_prev)
    for k in range(F):
        remote(b_send, b_recv.at[f], b_ss, b_rs, (to_dp, lax.rem(f + k, F)))
    b_cp = pltpu.make_async_remote_copy(
        src_ref=b_recv, dst_ref=b_recv, send_sem=b_ss, recv_sem=b_rs,
        device_id=(to_dp, f), device_id_type=MESH,
    )

    c2[0].wait_recv()
    fold(0)
    c2.append(halve(1))

    for n in range(1, levels - 1):
        c2[n].wait_recv()
        fold(n)
        c2.append(halve(n + 1))

    i_cp.wait_recv()
    inv = jnp.concatenate([i_buf[fsdp_slot(r)] for r in range(F)], axis=1)
    s2.wait_recv()
    logits = jnp.concatenate([s2_buf[fsdp_slot(r)] for r in range(F)], axis=1)
    exps = jnp.exp(logits)
    pooled = join3(nn(split3(exps), members[...]))
    b_cp.wait_recv()

    def column_of(rs):
        row = b_recv[rs[0]]
        for r in rs[1:]:
            row = row + b_recv[r]
        return jnp.sum(jnp.where(eye, row, 0.0), axis=1, keepdims=True)

    from_prev = column_of(range(F // 2, F))
    from_next = column_of(range(F // 2))
    pooled = pooled + from_prev * at_prev + from_next * at_next
    pooled = jnp.where(pooled > 0.0, pooled, 1.0)
    coef = jnp.log(pooled / lens_f)
    other = jnp.concatenate([coef[PAIRS:], coef[:PAIRS]], axis=0)
    row_of = lax.broadcasted_iota(jnp.int32, (8, prompts), 0)
    sign = jnp.where(row_of < PAIRS, -1.0, 1.0)
    margin = sign * (coef - other)
    softplus = jnp.maximum(margin, 0.0) + jnp.log1p(jnp.exp(-jnp.abs(margin)))
    loss_part = jnp.sum(jnp.where(row_of < PAIRS, softplus * owned, 0.0)) / n_battles
    ratio = sign * (1.0 / (1.0 + jnp.exp(-margin))) / n_battles / pooled
    grads = exps * join3(nt(split3(ratio), members[...]))
    slope = jnp.sum(grads * logits, axis=0, keepdims=True) * inv * inv / width
    grads = grads * inv

    for b in range(toks // LANES):
        lanes = slice(b * LANES, (b + 1) * LANES)
        id_blk = ids[:, lanes]
        full = jnp.zeros((wide, LANES), F32)
        for j in range(2 * PAIRS):
            full = full + jnp.where(model_of == id_blk[j : j + 1], grads[j : j + 1, lanes], 0.0)
        g_t[:, lanes] = full.astype(BF16)
    head_part = nn(g_t[...], hid[...])
    for t in range(tiles):
        g_tile[t] = head_part[16 * t : 16 * t + 16]
        g_send[t] = head_part[16 * t : 16 * t + 16].astype(BF16)
    for t in range(tiles, XY):
        g_tile[t] = jnp.zeros((16, dl), F32)
        g_send[t] = jnp.zeros((16, dl), BF16)
    s4 = scatter(g_send, s4_recv, s4_ss, s4_rs, xy_peer, xy_dev)

    c2[-1].wait_recv()
    tile = half[-1][0, bits[-1]].astype(F32) + half_recv[-1][0].astype(F32)
    c_blk = join3(nn(split3(jnp.exp(tile * inv)), members[...]))
    mine = jnp.where(f == tiles, loss_part, c_blk)
    c5_all[0] = mine
    c5 = gather(c5_all, c5_ss, c5_rs, xy_peer, xy_dev)

    c_rows = lax.broadcasted_iota(jnp.int32, (16, toks), 0)
    slope_hi = slope.astype(BF16).astype(F32)
    slope_lo = slope - slope_hi
    slope3 = jnp.where(c_rows == 0, slope_hi, jnp.where(c_rows == 1, slope_lo, 0.0)).astype(BF16)
    ones_w = jnp.ones((16, dl), BF16)
    outs = []
    for i in range(n_blk):
        rows = pl.ds(i * blk, blk)
        gn = tn(g_t[:, rows], wpad[...])
        cb = tn(slope3[:, i * blk : (i + 1) * blk], ones_w)
        out_v[rows, :] = (gain_v[...] * gn - hid[rows, :].astype(F32) * cb).astype(BF16)
        cp = pltpu.make_async_copy(out_v.at[rows], gh_out.at[rows], out_sem.at[i])
        cp.start()
        outs.append(cp)

    s4.wait_recv()
    total = g_tile[xy]
    for k in range(1, XY):
        total = total + s4_recv[k].astype(F32)
    s5_send[...] = total
    s5 = remote(s5_send, s5_recv, s5_ss, s5_rs, zh_dev)

    c5.wait_recv()
    csum = c5_all[xy_slot(0)]
    for q in range(1, XY):
        csum = csum + c5_all[xy_slot(q)]
    c5_sum[...] = csum
    c5b = remote(c5_sum, c5_other, c5b_ss, c5b_rs, zh_dev)

    s5.wait_recv()
    ag[0] = (s5_send[...] + s5_recv[...]).astype(BF16)
    s6 = gather(ag, s6_ss, s6_rs, xy_peer, xy_dev)

    c5b.wait_recv()
    csum = c5_sum[...] + c5_other[...]
    loss_hi = csum.astype(BF16).astype(F32)
    crow = lax.broadcasted_iota(jnp.int32, (16, prompts), 0)
    loss_blk = jnp.where(crow == 0, loss_hi, jnp.where(crow == 1, csum - loss_hi, 0.0))
    coef_blk = jnp.log(csum / lens_f)
    ctab[0] = jnp.where(f == tiles, loss_blk, coef_blk).astype(BF16)
    c6 = gather(ctab, c6_ss, c6_rs, fsdp_peer, fsdp_dev)

    def hand(n, src, dst):
        cp = pltpu.make_async_copy(src, dst, out_sem.at[n_blk + n])
        cp.start()
        outs.append(cp)

    s6.wait_recv()
    whole = jnp.concatenate([ag[xy_slot(t)].astype(F32) for t in range(tiles)], axis=0)
    ghead_v[...] = (gain_v[...] * whole)[:models]
    ggain_v[...] = jnp.sum(wpad[...].astype(F32) * whole, axis=0, keepdims=True)
    hand(0, ghead_v, ghead_out)
    hand(1, ggain_v, ggain_out)

    c6.wait_recv()
    table = jnp.concatenate([ctab[fsdp_slot(t)].astype(F32) for t in range(tiles)], axis=0)
    coef_v[...] = table[:models]
    loss_v[...] = jnp.sum(ctab[fsdp_slot(tiles)].astype(F32)[0:2, 0:1], axis=0, keepdims=True)
    hand(2, coef_v, coef_out)
    hand(3, loss_v, loss_out)

    for cp in [q_cp, i_cp, s1, s2, b_cp, s4, s5, s6, c1] + c2 + [c5, c5b, c6]:
        cp.wait_send()
    for cp in outs:
        cp.wait()


def hand_out(loss, coef, gh, ghead, ggain, loss_o, coef_o, gh_o, ghead_o, ggain_o, sems):
    rows = gh.shape[0] // 4
    pairs = [(gh.at[pl.ds(n * rows, rows)], gh_o.at[pl.ds(n * rows, rows)]) for n in range(4)]
    pairs += [(ghead, ghead_o), (coef, coef_o), (ggain, ggain_o), (loss, loss_o)]
    cps = [pltpu.make_async_copy(a, b, sems.at[n]) for n, (a, b) in enumerate(pairs)]
    for cp in cps:
        cp.start()
    for cp in cps:
        cp.wait()


def on_device(hidden, gain, head_weight, lengths, battles):
    toks, dl = hidden.shape
    models = head_weight.shape[0]
    prompts = lengths.shape[0]
    n_battles = battles.shape[0]
    tiles = -(-models // 16)
    wide = 16 * tiles
    blk = min(512, toks)
    levels = ZL.bit_length() - 1
    sem = pltpu.SemaphoreType.DMA
    hbm = pl.BlockSpec(memory_space=pl.ANY)
    V = pltpu.VMEM
    kinds = (
        ((1, 1), F32), ((models, prompts), F32), ((toks, dl), BF16), ((models, dl), F32), ((1, dl), F32)
    )
    operands = [hidden, gain.reshape(1, dl), head_weight, lengths.reshape(1, prompts), battles.T]
    operands = [pltpu.with_memory_space_constraint(a, pltpu.HBM) for a in operands]
    results = pl.pallas_call(
        functools.partial(kernel, models, float(dl * F), float(n_battles), blk),
        out_shape=tuple(pltpu.VMEM(*k) for k in kinds),
        in_specs=[hbm] * 5,
        out_specs=(hbm,) * 5,
        scratch_shapes=[
            V((toks, dl), BF16), V((1, dl), F32), V((models, dl), BF16),
            V((1, prompts), jnp.int32), V((2, n_battles), jnp.int32),
            V((wide, dl), BF16), V((wide, dl), BF16),
            V((toks, prompts), BF16), V((2 * PAIRS, toks), F32), V((wide, toks), F32),
            V((ZL, NC, 16, toks), BF16), V((toks, dl), BF16),
            V((1, 1), F32), V((models, prompts), F32), V((models, dl), F32), V((1, dl), F32),
            V((F, 1, LANES), F32), V((F, 1, LANES), F32), V((F, 1, LANES), F32),
            V((F, 8, LANES), F32), V((F, 8, LANES), F32), V((F, 8, LANES), F32),
            V((1, LANES), F32), V((F, 1, LANES), F32),
            V((wide, toks), BF16), V((XY, 16, dl), F32), V((XY, 16, dl), BF16),
            V((XY, 16, dl), BF16), V((16, dl), F32), V((16, dl), F32), V((XY, 16, dl), BF16),
            V((ZL, 16, toks), BF16),
            V((XY, 16, prompts), F32), V((16, prompts), F32), V((16, prompts), F32),
            V((F, 16, prompts), BF16),
            sem((4 + toks // blk,)), sem((4 + toks // blk,)),
            *[sem] * 18, sem((levels,)), sem((levels,)), *[sem] * 6,
        ]
        + [V((ZL >> (n + 1), 2, 16, toks), BF16) for n in range(levels)]
        + [V((ZL >> (n + 1), 16, toks), BF16) for n in range(levels)],
        compiler_params=pltpu.CompilerParams(
            collective_id=0, has_side_effects=True, vmem_limit_bytes=48 * 2**20
        ),
        name="head",
    )(*operands)
    loss, coef, gh, ghead, ggain = pl.pallas_call(
        hand_out,
        out_shape=tuple(pltpu.HBM(*k) for k in kinds),
        in_specs=[hbm] * 5,
        out_specs=(hbm,) * 5,
        scratch_shapes=[sem((8,))],
        compiler_params=pltpu.CompilerParams(vmem_limit_bytes=2**20),
        name="hand_out",
    )(*[pltpu.with_memory_space_constraint(a, pltpu.VMEM) for a in results])
    return loss.reshape(()), coef.T, gh, ghead, ggain.reshape(dl)


def solution(mesh):
    placed = (P("dp", "fsdp"), P("fsdp"), P(None, "fsdp"), P(), P())
    return jax.shard_map(
        on_device,
        mesh=mesh,
        in_specs=placed,
        out_specs=(P(), P(), P("dp", "fsdp"), P(None, "fsdp"), P("fsdp")),
        check_vma=False,
    )
```

```python
import functools

import jax
import jax.numpy as jnp
from jax import lax
from jax.experimental import pallas as pl
from jax.experimental.pallas import tpu as pltpu
from jax.sharding import PartitionSpec as P

Y, X, ZH, ZL, NC = 4, 4, 2, 8, 2
XY, F, DP, RING = Y * X, ZL * NC, Y * X * ZH, ZH * ZL
LANES = 128
PAIRS = 4
EPS = 1e-06
MESH = pl.DeviceIdType.MESH
F32, BF16 = jnp.float32, jnp.bfloat16


def nn(a, b):
    return lax.dot_general(a, b, (((1,), (0,)), ((), ())), preferred_element_type=F32)


def nt(a, b):
    return lax.dot_general(a, b, (((1,), (1,)), ((), ())), preferred_element_type=F32)


def tn(a, b):
    return lax.dot_general(a, b, (((0,), (0,)), ((), ())), preferred_element_type=F32)


def split3(x):
    hi = x.astype(BF16).astype(F32)
    mid = (x - hi).astype(BF16).astype(F32)
    return jnp.concatenate([hi, mid, x - hi - mid], axis=0).astype(BF16)


def join3(x):
    rows = x.shape[0] // 3
    return x[:rows] + x[rows : 2 * rows] + x[2 * rows :]


def kernel(
    models, width, n_battles, blk,
    hidden_hbm, gain_hbm, head_hbm, lens_hbm, battles_hbm,
    loss_out, coef_out, gh_out, ghead_out, ggain_out,
    hid, gain_v, head_v, lens_v, bat_v, wp, wpad, members, ids, raw, raw16, out_v,
    loss_v, coef_v, ghead_v, ggain_v,
    q_send, q_core, q_pair, q_recv, i_all, s1_send, s1_core, s1_pair, s1_recv, s2_all,
    b_send, b_core, b_sum, b_recv, g_t, g_tile, g_send, s4_recv,
    s5_send, s5_recv, ag, c1_recv, c5_all, ctab,
    load_sem, out_sem, qc_ss, qc_rs, q_ss, q_rs, i_ss, i_rs, ic_ss, ic_rs,
    s1c_ss, s1c_rs, s1_ss, s1_rs, s2_ss, s2_rs, s2c_ss, s2c_rs, bc_ss, bc_rs, b_ss, b_rs, s4_ss, s4_rs,
    s5_ss, s5_rs, s6_ss, s6_rs, c1_ss, c1_rs, c2_ss, c2_rs, c5_ss, c5_rs, c6_ss, c6_rs, c6c_ss, c6c_rs,
    *halves,
):
    toks, dl = hid.shape
    prompts = members.shape[1]
    tiles = -(-models // 16)
    levels = len(halves) // 2
    half, half_recv = halves[:levels], halves[levels:]
    dp = lax.axis_index("dp")
    f = lax.axis_index("fsdp")
    xy, zh = dp // ZH, dp % ZH
    y, x = xy // X, xy % X
    zl, c = f // NC, f % NC
    base = dp * toks

    def ring_peer(k):
        return lax.rem(zh * ZL + zl + k, RING)

    def ring_dev(r):
        return (xy * ZH + r // ZL, (r % ZL) * NC + c)

    def ring_slot(r):
        return lax.rem(zh * ZL + zl + RING - r, RING)

    def z_peer(k):
        return lax.rem(zl + k, ZL)

    def xy_peer(k):
        return lax.rem(y + k // X, Y) * X + lax.rem(x + k % X, X)

    def xy_dev(q):
        return (q * ZH + zh, f)

    core_dev = (dp, zl * NC + (1 - c))
    zh_dev = (xy * ZH + (1 - zh), f)
    dp_next, dp_prev = lax.rem(dp + 1, DP), lax.rem(dp + DP - 1, DP)

    loads = [
        pltpu.make_async_copy(lens_hbm, lens_v, load_sem.at[0]),
        pltpu.make_async_copy(battles_hbm, bat_v, load_sem.at[1]),
        pltpu.make_async_copy(gain_hbm, gain_v, load_sem.at[2]),
        pltpu.make_async_copy(head_hbm, head_v, load_sem.at[3]),
    ]
    n_blk = toks // blk
    for i in range(n_blk):
        rows = pl.ds(i * blk, blk)
        loads.append(pltpu.make_async_copy(hidden_hbm.at[rows], hid.at[rows], load_sem.at[4 + i]))
    for cp in loads:
        cp.start()

    barrier = pltpu.get_barrier_semaphore()
    partners = [core_dev] + [(dp, z_peer(k) * NC + c) for k in range(1, ZL)]
    partners += [xy_dev(xy_peer(k)) for k in range(1, XY)]
    partners += [((xy * ZH + (1 - zh)), r * NC + c) for r in range(ZL)]
    partners += [(dp_prev if r >= ZL // 2 else dp_next, r * NC + c) for r in range(ZL)]
    for dev in partners:
        pl.semaphore_signal(barrier, inc=1, device_id=dev, device_id_type=MESH)

    loads[0].wait()
    lens = jnp.broadcast_to(lens_v[...], (8, prompts))
    len_hi = lens // 32
    len_lo = lens - len_hi * 32
    upto = (
        lax.broadcasted_iota(jnp.int32, (prompts, prompts), 0)
        <= lax.broadcasted_iota(jnp.int32, (prompts, prompts), 1)
    ).astype(F32).astype(BF16)
    ends = (32.0 * nn(len_hi.astype(F32).astype(BF16), upto) + nn(len_lo.astype(F32).astype(BF16), upto))[:1]
    ends = ends.astype(jnp.int32)
    lens = lens[:1]
    starts = ends - lens
    lens_f = lens.astype(F32)
    at_prev = ((starts < base) & (ends > base)).astype(F32)
    at_next = ((starts < base + toks) & (ends > base + toks)).astype(F32)
    here = jnp.minimum(ends, base + toks) - jnp.maximum(starts, base)
    here = jnp.maximum(here, 0).astype(F32)
    first, last = starts // toks, (ends - 1) // toks
    in_first = jnp.where(first == last, lens, last * toks - starts)
    in_low = jnp.where(first % ZH == 0, in_first, lens - in_first)
    owned = ((ends > base) & (ends <= base + toks)).astype(F32)
    before_end = jnp.sum(at_prev * ends.astype(F32), axis=1, keepdims=True)
    from_start = jnp.sum(at_next * starts.astype(F32), axis=1, keepdims=True)
    from_start = jnp.where(jnp.sum(at_next, axis=1, keepdims=True) > 0.0, from_start, 2.0**30)

    loads[2].wait()
    loads[3].wait()
    wide = 16 * tiles
    head_f = head_v[...].astype(F32)
    if wide > models:
        head_f = jnp.concatenate([head_f, jnp.zeros((wide - models, dl), F32)], axis=0)
    wpad[...] = head_f.astype(BF16)
    wp[...] = (head_f * gain_v[...]).astype(BF16)

    def remote(src, dst, ss, rs, dev):
        cp = pltpu.make_async_remote_copy(
            src_ref=src, dst_ref=dst, send_sem=ss, recv_sem=rs, device_id=dev, device_id_type=MESH
        )
        cp.start()
        return cp

    def scatter(src, dst, ss, rs, peer, dev):
        for k in range(1, dst.shape[0]):
            remote(src.at[peer(k)], dst.at[k], ss, rs, dev(peer(k)))
        rest = dst.at[pl.ds(1, dst.shape[0] - 1)]
        return pltpu.make_async_remote_copy(
            src_ref=rest, dst_ref=rest, send_sem=ss, recv_sem=rs, device_id=dev(peer(1)), device_id_type=MESH
        )

    def gather(buf, ss, rs, peer, dev):
        for k in range(1, buf.shape[0]):
            remote(buf.at[0], buf.at[k], ss, rs, dev(peer(k)))
        rest = buf.at[pl.ds(1, buf.shape[0] - 1)]
        return pltpu.make_async_remote_copy(
            src_ref=rest, dst_ref=rest, send_sem=ss, recv_sem=rs, device_id=dev(peer(1)), device_id_type=MESH
        )

    def z_dev(r):
        return (dp, r * NC + c)

    def z_slot(r):
        return lax.rem(zl + ZL - r, ZL)

    def xy_slot(q):
        return lax.rem(y + Y - q // X, Y) * X + lax.rem(x + X - q % X, X)

    for t in range(tiles, ZL * NC):
        raw16[t // NC, t % NC] = jnp.zeros((16, toks), BF16)
    for i in range(n_blk):
        loads[4 + i].wait()
        rows = pl.ds(i * blk, blk)
        block = nt(wp[...], hid[rows, :])
        raw[:, rows] = block
        for t in range(tiles):
            raw16[t // NC, t % NC, :, rows] = block[16 * t : 16 * t + 16].astype(BF16)

    pl.semaphore_wait(barrier, len(partners))
    c1 = remote(raw16.at[:, 1 - c], c1_recv, c1_ss, c1_rs, (dp, zl * NC + (1 - c)))

    bits = [(zl >> n) % 2 for n in range(levels)]

    def halve(n):
        step = 1 << n
        peer = (zl + step - 2 * step * bits[n]) * NC + c
        return remote(half[n].at[:, 1 - bits[n]], half_recv[n], c2_ss.at[n], c2_rs.at[n], (dp, peer))

    def fold(n):
        for j in range(half_recv[n].shape[0]):
            total = half[n][j, bits[n]].astype(F32) + half_recv[n][j].astype(F32)
            half[n + 1][j // 2, j % 2] = total.astype(BF16)

    for i in range(n_blk):
        pos = base + i * blk + lax.broadcasted_iota(jnp.int32, (blk, prompts), 0)
        inside = (pos >= starts) & (pos < ends)
        members[pl.ds(i * blk, blk), :] = inside.astype(F32).astype(BF16)
    loads[1].wait()
    n_bat = bat_v.shape[1]
    bat_row = lax.broadcasted_iota(jnp.int32, (2 * PAIRS, n_bat), 0)
    bat_lane = lax.broadcasted_iota(jnp.int32, (2 * PAIRS, n_bat), 1)
    bat = jnp.where(bat_row < PAIRS, bat_v[0:1, :], bat_v[1:2, :])
    bat = jnp.where(bat_lane % PAIRS == bat_row % PAIRS, bat, 0)
    judged = lax.broadcasted_iota(jnp.int32, (n_bat, prompts), 0) // PAIRS
    judged = judged == lax.broadcasted_iota(jnp.int32, (n_bat, prompts), 1)
    bat = nn(bat.astype(F32).astype(BF16), judged.astype(F32).astype(BF16))
    ids[...] = nt(bat.astype(BF16), members[...])

    ones_l = jnp.ones((8, LANES), BF16)
    for i in range(n_blk):
        hf = hid[pl.ds(i * blk, blk), :].astype(F32)
        sq = hf * hf
        part = sq[:, :LANES]
        for j in range(1, dl // LANES):
            part = part + sq[:, j * LANES : (j + 1) * LANES]
        part_hi = part.astype(BF16)
        part_lo = (part - part_hi.astype(F32)).astype(BF16)
        sumsq = nt(ones_l, part_hi) + nt(ones_l, part_lo)
        for b in range(blk // LANES):
            dest = i * (blk // LANES) + b
            q_send[dest % NC, dest // NC] = sumsq[0:1, b * LANES : (b + 1) * LANES]
    qc = remote(q_send.at[1 - c], q_core, qc_ss, qc_rs, core_dev)

    model_of = lax.broadcasted_iota(jnp.int32, (wide, LANES), 0).astype(F32)
    for b in range(toks // LANES):
        lanes = slice(b * LANES, (b + 1) * LANES)
        id_blk = ids[:, lanes]
        found = [jnp.zeros((8, LANES), F32) for _ in range(2 * PAIRS)]
        for t in range(wide // 8):
            rows = slice(8 * t, 8 * t + 8)
            block, number = raw[rows, lanes], model_of[rows]
            found = [jnp.where(number == id_blk[j : j + 1], block, found[j]) for j in range(2 * PAIRS)]
        picked = [jnp.sum(one, axis=0, keepdims=True) for one in found]
        s1_send[b % NC, b // NC] = jnp.concatenate(picked, axis=0)

    s1c = remote(s1_send.at[1 - c], s1_core, s1c_ss, s1c_rs, core_dev)
    qc.wait_recv()
    q_pair[...] = q_send[c] + q_core[...]
    q_cp = scatter(q_pair, q_recv, q_ss, q_rs, z_peer, z_dev)
    c1.wait_recv()
    for k in range(ZL):
        half[0][k // 2, k % 2] = (raw16[k, c].astype(F32) + c1_recv[k].astype(F32)).astype(BF16)
    s1c.wait_recv()
    s1_pair[...] = s1_send[c] + s1_core[...]
    s1 = scatter(s1_pair, s1_recv, s1_ss, s1_rs, z_peer, z_dev)
    c2 = [halve(0)]


    q_cp.wait_recv()
    acc = q_pair[zl]
    for k in range(1, ZL):
        acc = acc + q_recv[k]
    inv_own = lax.rsqrt(acc / width + EPS)
    i_all[c, 0] = inv_own
    s1.wait_recv()
    acc = s1_pair[zl]
    for k in range(1, ZL):
        acc = acc + s1_recv[k]
    own = acc * inv_own
    s2_all[c, 0] = own
    s2 = gather(s2_all.at[c], s2_ss, s2_rs, z_peer, z_dev)
    i_cp = gather(i_all.at[c], i_ss, i_rs, z_peer, z_dev)

    late = f >= F // 2
    pos = base + f * LANES + lax.broadcasted_iota(jnp.int32, (8, LANES), 1)
    pos = pos.astype(F32)
    crossing = jnp.where(late, (pos >= from_start).astype(F32), (pos < before_end).astype(F32))
    column = jnp.sum(jnp.exp(own) * crossing, axis=1, keepdims=True)
    eye = lax.broadcasted_iota(jnp.int32, (8, LANES), 0) == lax.broadcasted_iota(jnp.int32, (8, LANES), 1)
    b_send[...] = jnp.sum(jnp.where(eye, column, 0.0), axis=0, keepdims=True)
    to_dp = jnp.where(late, dp_next, dp_prev)
    bc = remote(b_send, b_core, bc_ss, bc_rs, core_dev)
    bc.wait_recv()
    b_sum[...] = b_send[...] + b_core[...]
    for k in range(ZL):
        remote(b_sum, b_recv.at[zl], b_ss, b_rs, (to_dp, z_peer(k) * NC + c))
    b_cp = pltpu.make_async_remote_copy(
        src_ref=b_recv, dst_ref=b_recv, send_sem=b_ss, recv_sem=b_rs,
        device_id=(to_dp, f), device_id_type=MESH,
    )

    c2[0].wait_recv()
    fold(0)
    c2.append(halve(1))

    s2.wait_recv()
    s2c = remote(s2_all.at[c], s2_all.at[c], s2c_ss, s2c_rs, core_dev)
    i_cp.wait_recv()
    ic = remote(i_all.at[c], i_all.at[c], ic_ss, ic_rs, core_dev)
    for n in range(1, levels - 1):
        c2[n].wait_recv()
        fold(n)
        c2.append(halve(n + 1))

    s2c.wait_recv()
    ic.wait_recv()
    logits = jnp.concatenate([s2_all[r % NC, z_slot(r // NC)] for r in range(F)], axis=1)
    inv = jnp.concatenate([i_all[r % NC, z_slot(r // NC)] for r in range(F)], axis=1)
    exps = jnp.exp(logits)
    pooled = join3(nn(split3(exps), members[...]))
    b_cp.wait_recv()

    def column_of(rs):
        row = b_recv[rs[0]]
        for r in rs[1:]:
            row = row + b_recv[r]
        return jnp.sum(jnp.where(eye, row, 0.0), axis=1, keepdims=True)

    from_prev = column_of(range(ZL // 2, ZL))
    from_next = column_of(range(ZL // 2))
    pooled = pooled + from_prev * at_prev + from_next * at_next
    pooled = jnp.where(pooled > 0.0, pooled, 1.0)
    coef = jnp.log(pooled / lens_f)
    other = jnp.concatenate([coef[PAIRS:], coef[:PAIRS]], axis=0)
    row_of = lax.broadcasted_iota(jnp.int32, (8, prompts), 0)
    sign = jnp.where(row_of < PAIRS, -1.0, 1.0)
    margin = sign * (coef - other)
    softplus = jnp.maximum(margin, 0.0) + jnp.log1p(jnp.exp(-jnp.abs(margin)))
    loss_part = jnp.sum(jnp.where(row_of < PAIRS, softplus * owned, 0.0)) / n_battles
    ratio = sign * (1.0 / (1.0 + jnp.exp(-margin))) / n_battles / pooled
    grads = exps * join3(nt(split3(ratio), members[...]))
    slope = jnp.sum(grads * logits, axis=0, keepdims=True) * inv * inv / width
    grads = grads * inv

    for b in range(toks // LANES):
        lanes = slice(b * LANES, (b + 1) * LANES)
        id_blk = ids[:, lanes]
        g_blk = grads[:, lanes]
        same = jnp.zeros((8, LANES), F32)
        for j in range(2 * PAIRS):
            same = same + jnp.where(id_blk == id_blk[j : j + 1], g_blk[j : j + 1], 0.0)
        for t in range(wide // 16):
            rows = slice(16 * t, 16 * t + 16)
            full = jnp.zeros((16, LANES), F32)
            for j in range(2 * PAIRS):
                full = jnp.where(model_of[rows] == id_blk[j : j + 1], same[j : j + 1], full)
            g_t[rows, lanes] = full.astype(BF16)
    head_part = nn(g_t[...], hid[...])
    for t in range(tiles):
        g_tile[t] = head_part[16 * t : 16 * t + 16]
        g_send[t] = head_part[16 * t : 16 * t + 16].astype(BF16)
    for t in range(tiles, XY):
        g_tile[t] = jnp.zeros((16, dl), F32)
        g_send[t] = jnp.zeros((16, dl), BF16)
    s4 = scatter(g_send, s4_recv, s4_ss, s4_rs, xy_peer, xy_dev)

    c2[-1].wait_recv()
    tile = half[-1][0, bits[-1]].astype(F32) + half_recv[-1][0].astype(F32)
    c_blk = join3(nn(split3(jnp.exp(tile * inv)), members[...]))
    local = jnp.log(jnp.where(here > 0.0, c_blk, 1.0) / jnp.maximum(here, 1.0))
    crow = lax.broadcasted_iota(jnp.int32, (16, prompts), 0)

    def loss_rows(total):
        hi = total.astype(BF16).astype(F32)
        mid = (total - hi).astype(BF16).astype(F32)
        return jnp.where(crow == 0, hi, jnp.where(crow == 1, mid, jnp.where(crow == 2, total - hi - mid, 0.0)))

    loss_part = jnp.broadcast_to(loss_part, (16, prompts))
    mine = jnp.where(f == tiles, loss_rows(loss_part), local).astype(BF16)
    c5_all[0] = mine
    c5 = gather(c5_all, c5_ss, c5_rs, xy_peer, xy_dev)

    s4.wait_recv()
    total = g_tile[xy]
    for k in range(1, XY):
        total = total + s4_recv[k].astype(F32)
    s5_send[...] = total
    s5 = remote(s5_send, s5_recv, s5_ss, s5_rs, zh_dev)

    c5.wait_recv()
    csum = c5_all[xy_slot(0)].astype(F32)
    for q in range(1, XY):
        csum = csum + c5_all[xy_slot(q)].astype(F32)
    csum = jnp.where(f == tiles, loss_rows(csum[0:1] + csum[1:2] + csum[2:3]), csum)
    ctab[c, 0] = csum.astype(BF16)
    c6 = gather(ctab.at[c], c6_ss, c6_rs, ring_peer, ring_dev)

    c_rows = lax.broadcasted_iota(jnp.int32, (16, toks), 0)
    slope_hi = slope.astype(BF16).astype(F32)
    slope_lo = slope - slope_hi
    slope3 = jnp.where(c_rows == 0, slope_hi, jnp.where(c_rows == 1, slope_lo, 0.0)).astype(BF16)
    ones_w = jnp.ones((16, dl), BF16)
    outs = []
    for i in range(n_blk):
        rows = pl.ds(i * blk, blk)
        gn = tn(g_t[:, rows], wpad[...])
        cb = tn(slope3[:, i * blk : (i + 1) * blk], ones_w)
        out_v[rows, :] = (gain_v[...] * gn - hid[rows, :].astype(F32) * cb).astype(BF16)
        cp = pltpu.make_async_copy(out_v.at[rows], gh_out.at[rows], out_sem.at[i])
        cp.start()
        outs.append(cp)

    s5.wait_recv()
    ag[0] = (s5_send[...] + s5_recv[...]).astype(BF16)
    s6 = gather(ag, s6_ss, s6_rs, xy_peer, xy_dev)

    def hand(n, src, dst):
        cp = pltpu.make_async_copy(src, dst, out_sem.at[n_blk + n])
        cp.start()
        outs.append(cp)

    c6.wait_recv()
    c6c = remote(ctab.at[c], ctab.at[c], c6c_ss, c6c_rs, core_dev)
    s6.wait_recv()
    whole = jnp.concatenate([ag[xy_slot(t)].astype(F32) for t in range(tiles)], axis=0)
    ghead_v[...] = (gain_v[...] * whole)[:models]
    ggain_v[...] = jnp.sum(wpad[...].astype(F32) * whole, axis=0, keepdims=True)
    hand(0, ghead_v, ghead_out)
    hand(1, ggain_v, ggain_out)

    c6c.wait_recv()

    def slot_of(half_at, t):
        return ctab[t % NC, ring_slot(half_at * ZL + t // NC)].astype(F32)

    low, high = (jnp.concatenate([slot_of(n, t) for t in range(tiles)], axis=0) for n in range(ZH))
    low_share = in_low.astype(F32) / lens_f
    high_share = (lens - in_low).astype(F32) / lens_f
    table = jnp.log(low_share * jnp.exp(low) + high_share * jnp.exp(high))
    table = jnp.where(in_low == lens, low, jnp.where(in_low == 0, high, table))
    coef_v[...] = table[:models]
    loss_all = slot_of(0, tiles) + slot_of(1, tiles)
    loss_v[...] = jnp.sum(loss_all[0:3, 0:1], axis=0, keepdims=True)
    hand(2, coef_v, coef_out)
    hand(3, loss_v, loss_out)

    for cp in [qc, q_cp, i_cp, ic, s1c, s1, s2, s2c, bc, b_cp, s4, s5, s6, c1] + c2 + [c5, c6, c6c]:
        cp.wait_send()
    for cp in outs:
        cp.wait()


def hand_out(loss, coef, gh, ghead, ggain, loss_o, coef_o, gh_o, ghead_o, ggain_o, sems):
    rows = gh.shape[0] // 4
    pairs = [(gh.at[pl.ds(n * rows, rows)], gh_o.at[pl.ds(n * rows, rows)]) for n in range(4)]
    pairs += [(ghead, ghead_o), (coef, coef_o), (ggain, ggain_o), (loss, loss_o)]
    cps = [pltpu.make_async_copy(a, b, sems.at[n]) for n, (a, b) in enumerate(pairs)]
    for cp in cps:
        cp.start()
    for cp in cps:
        cp.wait()


def on_device(hidden, gain, head_weight, lengths, battles):
    toks, dl = hidden.shape
    models = head_weight.shape[0]
    prompts = lengths.shape[0]
    n_battles = battles.shape[0]
    tiles = -(-models // 16)
    wide = 16 * tiles
    blk = min(512, toks)
    levels = ZL.bit_length() - 1
    sem = pltpu.SemaphoreType.DMA
    hbm = pl.BlockSpec(memory_space=pl.ANY)
    V = pltpu.VMEM
    kinds = (
        ((1, 1), F32), ((models, prompts), F32), ((toks, dl), BF16), ((models, dl), F32), ((1, dl), F32)
    )
    operands = [hidden, gain.reshape(1, dl), head_weight, lengths.reshape(1, prompts), battles.T]
    operands = [pltpu.with_memory_space_constraint(a, pltpu.HBM) for a in operands]
    results = pl.pallas_call(
        functools.partial(kernel, models, float(dl * F), float(n_battles), blk),
        out_shape=tuple(pltpu.VMEM(*k) for k in kinds),
        in_specs=[hbm] * 5,
        out_specs=(hbm,) * 5,
        scratch_shapes=[
            V((toks, dl), BF16), V((1, dl), F32), V((models, dl), BF16),
            V((1, prompts), jnp.int32), V((2, n_battles), jnp.int32),
            V((wide, dl), BF16), V((wide, dl), BF16),
            V((toks, prompts), BF16), V((2 * PAIRS, toks), F32), V((wide, toks), F32),
            V((ZL, NC, 16, toks), BF16), V((toks, dl), BF16),
            V((1, 1), F32), V((models, prompts), F32), V((models, dl), F32), V((1, dl), F32),
            V((NC, ZL, 1, LANES), F32), *[V((ZL, 1, LANES), F32)] * 3, V((NC, ZL, 1, LANES), F32),
            V((NC, ZL, 8, LANES), F32), *[V((ZL, 8, LANES), F32)] * 3, V((NC, ZL, 8, LANES), F32),
            *[V((1, LANES), F32)] * 3, V((ZL, 1, LANES), F32),
            V((wide, toks), BF16), V((XY, 16, dl), F32), V((XY, 16, dl), BF16),
            V((XY, 16, dl), BF16), V((16, dl), F32), V((16, dl), F32), V((XY, 16, dl), BF16),
            V((ZL, 16, toks), BF16),
            V((XY, 16, prompts), BF16), V((NC, RING, 16, prompts), BF16),
            sem((4 + toks // blk,)), sem((4 + toks // blk,)),
            *[sem] * 28, sem((levels,)), sem((levels,)), *[sem] * 6,
        ]
        + [V((ZL >> (n + 1), 2, 16, toks), BF16) for n in range(levels)]
        + [V((ZL >> (n + 1), 16, toks), BF16) for n in range(levels)],
        compiler_params=pltpu.CompilerParams(
            collective_id=0, has_side_effects=True, vmem_limit_bytes=48 * 2**20
        ),
        name="head",
    )(*operands)
    loss, coef, gh, ghead, ggain = pl.pallas_call(
        hand_out,
        out_shape=tuple(pltpu.HBM(*k) for k in kinds),
        in_specs=[hbm] * 5,
        out_specs=(hbm,) * 5,
        scratch_shapes=[sem((8,))],
        compiler_params=pltpu.CompilerParams(vmem_limit_bytes=2**20),
        name="hand_out",
    )(*[pltpu.with_memory_space_constraint(a, pltpu.VMEM) for a in results])
    return loss.reshape(()), coef.T, gh, ghead, ggain.reshape(dl)


def solution(mesh):
    placed = (P("dp", "fsdp"), P("fsdp"), P(None, "fsdp"), P(), P())
    return jax.shard_map(
        on_device,
        mesh=mesh,
        in_specs=placed,
        out_specs=(P(), P(), P("dp", "fsdp"), P(None, "fsdp"), P("fsdp")),
        check_vma=False,
    )
```

```python
import functools

import jax
import jax.numpy as jnp
from jax import lax
from jax.experimental import pallas as pl
from jax.experimental.pallas import tpu as pltpu
from jax.sharding import PartitionSpec as P

Y, X, ZH, ZL, NC = 4, 4, 2, 8, 2
XY, F, DP, RING = Y * X, ZL * NC, Y * X * ZH, ZH * ZL
LANES = 128
PAIRS = 4
EPS = 1e-06
MESH = pl.DeviceIdType.MESH
F32, BF16 = jnp.float32, jnp.bfloat16


def nn(a, b):
    return lax.dot_general(a, b, (((1,), (0,)), ((), ())), preferred_element_type=F32)


def nt(a, b):
    return lax.dot_general(a, b, (((1,), (1,)), ((), ())), preferred_element_type=F32)


def tn(a, b):
    return lax.dot_general(a, b, (((0,), (0,)), ((), ())), preferred_element_type=F32)


def split3(x):
    hi = x.astype(BF16).astype(F32)
    mid = (x - hi).astype(BF16).astype(F32)
    return jnp.concatenate([hi, mid, x - hi - mid], axis=0).astype(BF16)


def join3(x):
    rows = x.shape[0] // 3
    return x[:rows] + x[rows : 2 * rows] + x[2 * rows :]


def kernel(
    models, width, n_battles, blk,
    hidden_hbm, gain_hbm, head_hbm, lens_hbm, battles_hbm,
    loss_out, coef_out, gh_out, ghead_out, ggain_out,
    hid, gain_v, head_v, lens_v, bat_v, wp, wpad, members, ids, raw, raw16, out_v,
    loss_v, coef_v, ghead_v, ggain_v,
    q_send, q_core, q_pair, q_recv, i_all, s1_send, s1_core, s1_pair, s1_recv, s2_all,
    b_send, b_core, b_sum, b_recv, g_t, g_tile, g_send, s4_recv,
    s5_send, s5_recv, ag, c1_recv, c5_all, ctab,
    load_sem, out_sem, qc_ss, qc_rs, q_ss, q_rs, i_ss, i_rs, ic_ss, ic_rs,
    s1c_ss, s1c_rs, s1_ss, s1_rs, s2_ss, s2_rs, s2c_ss, s2c_rs, bc_ss, bc_rs, b_ss, b_rs, s4_ss, s4_rs,
    s5_ss, s5_rs, s6_ss, s6_rs, c1_ss, c1_rs, c2_ss, c2_rs, c5_ss, c5_rs, c6_ss, c6_rs, c6c_ss, c6c_rs,
    *halves,
):
    toks, dl = hid.shape
    prompts = members.shape[1]
    tiles = -(-models // 16)
    levels = len(halves) // 2
    half, half_recv = halves[:levels], halves[levels:]
    dp = lax.axis_index("dp")
    f = lax.axis_index("fsdp")
    xy, zh = dp // ZH, dp % ZH
    y, x = xy // X, xy % X
    zl, c = f // NC, f % NC
    base = dp * toks

    def ring_peer(k):
        return lax.rem(zh * ZL + zl + k, RING)

    def ring_dev(r):
        return (xy * ZH + r // ZL, (r % ZL) * NC + c)

    def ring_slot(r):
        return lax.rem(zh * ZL + zl + RING - r, RING)

    def z_peer(k):
        return lax.rem(zl + k, ZL)

    def xy_peer(k):
        return lax.rem(y + k // X, Y) * X + lax.rem(x + k % X, X)

    def xy_dev(q):
        return (q * ZH + zh, f)

    core_dev = (dp, zl * NC + (1 - c))
    zh_dev = (xy * ZH + (1 - zh), f)
    dp_next, dp_prev = lax.rem(dp + 1, DP), lax.rem(dp + DP - 1, DP)

    barrier = pltpu.get_barrier_semaphore()
    partners = [core_dev] + [(dp, z_peer(k) * NC + c) for k in range(1, ZL)]
    partners += [xy_dev(xy_peer(k)) for k in range(1, XY)]
    partners += [((xy * ZH + (1 - zh)), r * NC + c) for r in range(ZL)]
    partners += [(dp_prev if r >= ZL // 2 else dp_next, r * NC + c) for r in range(ZL)]
    for dev in partners[::-1]:
        pl.semaphore_signal(barrier, inc=1, device_id=dev, device_id_type=MESH)

    loads = [
        pltpu.make_async_copy(lens_hbm, lens_v, load_sem.at[0]),
        pltpu.make_async_copy(battles_hbm, bat_v, load_sem.at[1]),
        pltpu.make_async_copy(gain_hbm, gain_v, load_sem.at[2]),
        pltpu.make_async_copy(head_hbm, head_v, load_sem.at[3]),
    ]
    n_blk = toks // blk
    for i in range(n_blk):
        rows = pl.ds(i * blk, blk)
        loads.append(pltpu.make_async_copy(hidden_hbm.at[rows], hid.at[rows], load_sem.at[4 + i]))
    for cp in loads:
        cp.start()

    loads[0].wait()
    lens = jnp.broadcast_to(lens_v[...], (8, prompts))
    len_hi = lens // 32
    len_lo = lens - len_hi * 32
    upto = (
        lax.broadcasted_iota(jnp.int32, (prompts, prompts), 0)
        <= lax.broadcasted_iota(jnp.int32, (prompts, prompts), 1)
    ).astype(F32).astype(BF16)
    ends = (32.0 * nn(len_hi.astype(F32).astype(BF16), upto) + nn(len_lo.astype(F32).astype(BF16), upto))[:1]
    ends = ends.astype(jnp.int32)
    lens = lens[:1]
    starts = ends - lens
    lens_f = lens.astype(F32)
    at_prev = ((starts < base) & (ends > base)).astype(F32)
    at_next = ((starts < base + toks) & (ends > base + toks)).astype(F32)
    here = jnp.minimum(ends, base + toks) - jnp.maximum(starts, base)
    here = jnp.maximum(here, 0).astype(F32)
    first, last = starts // toks, (ends - 1) // toks
    in_first = jnp.where(first == last, lens, last * toks - starts)
    in_low = jnp.where(first % ZH == 0, in_first, lens - in_first)
    owned = ((ends > base) & (ends <= base + toks)).astype(F32)
    before_end = jnp.sum(at_prev * ends.astype(F32), axis=1, keepdims=True)
    from_start = jnp.sum(at_next * starts.astype(F32), axis=1, keepdims=True)
    from_start = jnp.where(jnp.sum(at_next, axis=1, keepdims=True) > 0.0, from_start, 2.0**30)

    loads[2].wait()
    loads[3].wait()
    wide = 16 * tiles
    head_f = head_v[...].astype(F32)
    if wide > models:
        head_f = jnp.concatenate([head_f, jnp.zeros((wide - models, dl), F32)], axis=0)
    wpad[...] = head_f.astype(BF16)
    wp[...] = (head_f * gain_v[...]).astype(BF16)

    def remote(src, dst, ss, rs, dev):
        cp = pltpu.make_async_remote_copy(
            src_ref=src, dst_ref=dst, send_sem=ss, recv_sem=rs, device_id=dev, device_id_type=MESH
        )
        cp.start()
        return cp

    def scatter(src, dst, ss, rs, peer, dev):
        for k in range(1, dst.shape[0]):
            remote(src.at[peer(k)], dst.at[k], ss, rs, dev(peer(k)))
        rest = dst.at[pl.ds(1, dst.shape[0] - 1)]
        return pltpu.make_async_remote_copy(
            src_ref=rest, dst_ref=rest, send_sem=ss, recv_sem=rs, device_id=dev(peer(1)), device_id_type=MESH
        )

    def gather(buf, ss, rs, peer, dev):
        for k in range(1, buf.shape[0]):
            remote(buf.at[0], buf.at[k], ss, rs, dev(peer(k)))
        rest = buf.at[pl.ds(1, buf.shape[0] - 1)]
        return pltpu.make_async_remote_copy(
            src_ref=rest, dst_ref=rest, send_sem=ss, recv_sem=rs, device_id=dev(peer(1)), device_id_type=MESH
        )

    def z_dev(r):
        return (dp, r * NC + c)

    def z_slot(r):
        return lax.rem(zl + ZL - r, ZL)

    def xy_slot(q):
        return lax.rem(y + Y - q // X, Y) * X + lax.rem(x + X - q % X, X)

    for t in range(tiles, ZL * NC):
        raw16[t // NC, t % NC] = jnp.zeros((16, toks), BF16)
    for i in range(n_blk):
        loads[4 + i].wait()
        rows = pl.ds(i * blk, blk)
        block = nt(wp[...], hid[rows, :])
        raw[:, rows] = block
        for t in range(tiles):
            raw16[t // NC, t % NC, :, rows] = block[16 * t : 16 * t + 16].astype(BF16)

    bits = [(zl >> n) % 2 for n in range(levels)]

    def halve(n):
        step = 1 << n
        peer = (zl + step - 2 * step * bits[n]) * NC + c
        return remote(half[n].at[:, 1 - bits[n]], half_recv[n], c2_ss.at[n], c2_rs.at[n], (dp, peer))

    def fold(n):
        for j in range(half_recv[n].shape[0]):
            total = half[n][j, bits[n]].astype(F32) + half_recv[n][j].astype(F32)
            half[n + 1][j // 2, j % 2] = total.astype(BF16)

    for i in range(n_blk):
        pos = base + i * blk + lax.broadcasted_iota(jnp.int32, (blk, prompts), 0)
        inside = (pos >= starts) & (pos < ends)
        members[pl.ds(i * blk, blk), :] = inside.astype(F32).astype(BF16)
    loads[1].wait()
    n_bat = bat_v.shape[1]
    bat_row = lax.broadcasted_iota(jnp.int32, (2 * PAIRS, n_bat), 0)
    bat_lane = lax.broadcasted_iota(jnp.int32, (2 * PAIRS, n_bat), 1)
    bat = jnp.where(bat_row < PAIRS, bat_v[0:1, :], bat_v[1:2, :])
    bat = jnp.where(bat_lane % PAIRS == bat_row % PAIRS, bat, 0)
    judged = lax.broadcasted_iota(jnp.int32, (n_bat, prompts), 0) // PAIRS
    judged = judged == lax.broadcasted_iota(jnp.int32, (n_bat, prompts), 1)
    bat = nn(bat.astype(F32).astype(BF16), judged.astype(F32).astype(BF16))
    ids[...] = nt(bat.astype(BF16), members[...])

    ones_l = jnp.ones((8, LANES), BF16)
    for i in range(n_blk):
        hf = hid[pl.ds(i * blk, blk), :].astype(F32)
        sq = hf * hf
        part = sq[:, :LANES]
        for j in range(1, dl // LANES):
            part = part + sq[:, j * LANES : (j + 1) * LANES]
        part_hi = part.astype(BF16)
        part_lo = (part - part_hi.astype(F32)).astype(BF16)
        sumsq = nt(ones_l, part_hi) + nt(ones_l, part_lo)
        for b in range(blk // LANES):
            dest = i * (blk // LANES) + b
            q_send[dest % NC, dest // NC] = sumsq[0:1, b * LANES : (b + 1) * LANES]
    model_of = lax.broadcasted_iota(jnp.int32, (wide, LANES), 0).astype(F32)
    for b in range(toks // LANES):
        lanes = slice(b * LANES, (b + 1) * LANES)
        id_blk = ids[:, lanes]
        found = [jnp.zeros((8, LANES), F32) for _ in range(2 * PAIRS)]
        for t in range(wide // 8):
            rows = slice(8 * t, 8 * t + 8)
            block, number = raw[rows, lanes], model_of[rows]
            found = [jnp.where(number == id_blk[j : j + 1], block, found[j]) for j in range(2 * PAIRS)]
        picked = [jnp.sum(one, axis=0, keepdims=True) for one in found]
        s1_send[b % NC, b // NC] = jnp.concatenate(picked, axis=0)

    pl.semaphore_wait(barrier, len(partners))
    s1c = remote(s1_send.at[1 - c], s1_core, s1c_ss, s1c_rs, core_dev)
    qc = remote(q_send.at[1 - c], q_core, qc_ss, qc_rs, core_dev)
    c1 = remote(raw16.at[:, 1 - c], c1_recv, c1_ss, c1_rs, (dp, zl * NC + (1 - c)))

    s1c.wait_recv()
    s1_pair[...] = s1_send[c] + s1_core[...]
    s1 = scatter(s1_pair, s1_recv, s1_ss, s1_rs, z_peer, z_dev)
    qc.wait_recv()
    q_pair[...] = q_send[c] + q_core[...]
    q_cp = scatter(q_pair, q_recv, q_ss, q_rs, z_peer, z_dev)
    c1.wait_recv()
    for k in range(ZL):
        half[0][k // 2, k % 2] = (raw16[k, c].astype(F32) + c1_recv[k].astype(F32)).astype(BF16)
    c2 = [halve(0)]


    q_cp.wait_recv()
    acc = q_pair[zl]
    for k in range(1, ZL):
        acc = acc + q_recv[k]
    inv_own = lax.rsqrt(acc / width + EPS)
    i_all[c, 0] = inv_own
    s1.wait_recv()
    acc = s1_pair[zl]
    for k in range(1, ZL):
        acc = acc + s1_recv[k]
    own = acc * inv_own
    s2_all[c, 0] = own
    s2 = gather(s2_all.at[c], s2_ss, s2_rs, z_peer, z_dev)
    i_cp = gather(i_all.at[c], i_ss, i_rs, z_peer, z_dev)

    late = f >= F // 2
    pos = base + f * LANES + lax.broadcasted_iota(jnp.int32, (8, LANES), 1)
    pos = pos.astype(F32)
    crossing = jnp.where(late, (pos >= from_start).astype(F32), (pos < before_end).astype(F32))
    column = jnp.sum(jnp.exp(own) * crossing, axis=1, keepdims=True)
    eye = lax.broadcasted_iota(jnp.int32, (8, LANES), 0) == lax.broadcasted_iota(jnp.int32, (8, LANES), 1)
    b_send[...] = jnp.sum(jnp.where(eye, column, 0.0), axis=0, keepdims=True)
    to_dp = jnp.where(late, dp_next, dp_prev)
    bc = remote(b_send, b_core, bc_ss, bc_rs, core_dev)
    bc.wait_recv()
    b_sum[...] = b_send[...] + b_core[...]
    for k in range(ZL):
        remote(b_sum, b_recv.at[zl], b_ss, b_rs, (to_dp, z_peer(k) * NC + c))
    b_cp = pltpu.make_async_remote_copy(
        src_ref=b_recv, dst_ref=b_recv, send_sem=b_ss, recv_sem=b_rs,
        device_id=(to_dp, f), device_id_type=MESH,
    )

    c2[0].wait_recv()
    fold(0)
    c2.append(halve(1))

    s2.wait_recv()
    s2c = remote(s2_all.at[c], s2_all.at[c], s2c_ss, s2c_rs, core_dev)
    i_cp.wait_recv()
    ic = remote(i_all.at[c], i_all.at[c], ic_ss, ic_rs, core_dev)
    for n in range(1, levels - 1):
        c2[n].wait_recv()
        fold(n)
        c2.append(halve(n + 1))

    s2c.wait_recv()
    ic.wait_recv()
    logits = jnp.concatenate([s2_all[r % NC, z_slot(r // NC)] for r in range(F)], axis=1)
    inv = jnp.concatenate([i_all[r % NC, z_slot(r // NC)] for r in range(F)], axis=1)
    exps = jnp.exp(logits)
    pooled = join3(nn(split3(exps), members[...]))
    b_cp.wait_recv()

    def column_of(rs):
        row = b_recv[rs[0]]
        for r in rs[1:]:
            row = row + b_recv[r]
        return jnp.sum(jnp.where(eye, row, 0.0), axis=1, keepdims=True)

    from_prev = column_of(range(ZL // 2, ZL))
    from_next = column_of(range(ZL // 2))
    pooled = pooled + from_prev * at_prev + from_next * at_next
    pooled = jnp.where(pooled > 0.0, pooled, 1.0)
    coef = jnp.log(pooled / lens_f)
    other = jnp.concatenate([coef[PAIRS:], coef[:PAIRS]], axis=0)
    row_of = lax.broadcasted_iota(jnp.int32, (8, prompts), 0)
    sign = jnp.where(row_of < PAIRS, -1.0, 1.0)
    margin = sign * (coef - other)
    softplus = jnp.maximum(margin, 0.0) + jnp.log1p(jnp.exp(-jnp.abs(margin)))
    loss_part = jnp.sum(jnp.where(row_of < PAIRS, softplus * owned, 0.0)) / n_battles
    ratio = sign * (1.0 / (1.0 + jnp.exp(-margin))) / n_battles / pooled
    grads = exps * join3(nt(split3(ratio), members[...]))
    slope = jnp.sum(grads * logits, axis=0, keepdims=True) * inv * inv / width
    grads = grads * inv

    for b in range(toks // LANES):
        lanes = slice(b * LANES, (b + 1) * LANES)
        id_blk = ids[:, lanes]
        g_blk = grads[:, lanes]
        same = jnp.zeros((8, LANES), F32)
        for j in range(2 * PAIRS):
            same = same + jnp.where(id_blk == id_blk[j : j + 1], g_blk[j : j + 1], 0.0)
        for t in range(wide // 16):
            rows = slice(16 * t, 16 * t + 16)
            full = jnp.zeros((16, LANES), F32)
            for j in range(2 * PAIRS):
                full = jnp.where(model_of[rows] == id_blk[j : j + 1], same[j : j + 1], full)
            g_t[rows, lanes] = full.astype(BF16)
    head_part = nn(g_t[...], hid[...])
    for t in range(tiles):
        g_tile[t] = head_part[16 * t : 16 * t + 16]
        g_send[t] = head_part[16 * t : 16 * t + 16].astype(BF16)
    for t in range(tiles, XY):
        g_tile[t] = jnp.zeros((16, dl), F32)
        g_send[t] = jnp.zeros((16, dl), BF16)
    s4 = scatter(g_send, s4_recv, s4_ss, s4_rs, xy_peer, xy_dev)

    c2[-1].wait_recv()
    tile = half[-1][0, bits[-1]].astype(F32) + half_recv[-1][0].astype(F32)
    c_blk = join3(nn(split3(jnp.exp(tile * inv)), members[...]))
    local = jnp.log(jnp.where(here > 0.0, c_blk, 1.0) / jnp.maximum(here, 1.0))
    crow = lax.broadcasted_iota(jnp.int32, (16, prompts), 0)

    def loss_rows(total):
        hi = total.astype(BF16).astype(F32)
        mid = (total - hi).astype(BF16).astype(F32)
        return jnp.where(crow == 0, hi, jnp.where(crow == 1, mid, jnp.where(crow == 2, total - hi - mid, 0.0)))

    loss_part = jnp.broadcast_to(loss_part, (16, prompts))
    mine = jnp.where(f == tiles, loss_rows(loss_part), local).astype(BF16)
    c5_all[0] = mine
    c5 = gather(c5_all, c5_ss, c5_rs, xy_peer, xy_dev)

    s4.wait_recv()
    total = g_tile[xy]
    for k in range(1, XY):
        total = total + s4_recv[k].astype(F32)
    s5_send[...] = total
    s5 = remote(s5_send, s5_recv, s5_ss, s5_rs, zh_dev)

    c5.wait_recv()
    csum = c5_all[xy_slot(0)].astype(F32)
    for q in range(1, XY):
        csum = csum + c5_all[xy_slot(q)].astype(F32)
    csum = jnp.where(f == tiles, loss_rows(csum[0:1] + csum[1:2] + csum[2:3]), csum)
    ctab[c, 0] = csum.astype(BF16)
    c6 = gather(ctab.at[c], c6_ss, c6_rs, ring_peer, ring_dev)

    c_rows = lax.broadcasted_iota(jnp.int32, (16, toks), 0)
    slope_hi = slope.astype(BF16).astype(F32)
    slope_lo = slope - slope_hi
    slope3 = jnp.where(c_rows == 0, slope_hi, jnp.where(c_rows == 1, slope_lo, 0.0)).astype(BF16)
    ones_w = jnp.ones((16, dl), BF16)
    outs = []
    for i in range(n_blk):
        rows = pl.ds(i * blk, blk)
        gn = tn(g_t[:, rows], wpad[...])
        cb = tn(slope3[:, i * blk : (i + 1) * blk], ones_w)
        out_v[rows, :] = (gain_v[...] * gn - hid[rows, :].astype(F32) * cb).astype(BF16)
        cp = pltpu.make_async_copy(out_v.at[rows], gh_out.at[rows], out_sem.at[i])
        cp.start()
        outs.append(cp)

    s5.wait_recv()
    ag[0] = (s5_send[...] + s5_recv[...]).astype(BF16)
    s6 = gather(ag, s6_ss, s6_rs, xy_peer, xy_dev)

    def hand(n, src, dst):
        cp = pltpu.make_async_copy(src, dst, out_sem.at[n_blk + n])
        cp.start()
        outs.append(cp)

    c6.wait_recv()
    c6c = remote(ctab.at[c], ctab.at[c], c6c_ss, c6c_rs, core_dev)
    s6.wait_recv()
    whole = jnp.concatenate([ag[xy_slot(t)].astype(F32) for t in range(tiles)], axis=0)
    ghead_v[...] = (gain_v[...] * whole)[:models]
    ggain_v[...] = jnp.sum(wpad[...].astype(F32) * whole, axis=0, keepdims=True)
    hand(0, ghead_v, ghead_out)
    hand(1, ggain_v, ggain_out)

    c6c.wait_recv()

    def slot_of(half_at, t):
        return ctab[t % NC, ring_slot(half_at * ZL + t // NC)].astype(F32)

    low, high = (jnp.concatenate([slot_of(n, t) for t in range(tiles)], axis=0) for n in range(ZH))
    low_share = in_low.astype(F32) / lens_f
    high_share = (lens - in_low).astype(F32) / lens_f
    table = jnp.log(low_share * jnp.exp(low) + high_share * jnp.exp(high))
    table = jnp.where(in_low == lens, low, jnp.where(in_low == 0, high, table))
    coef_v[...] = table[:models]
    loss_all = slot_of(0, tiles) + slot_of(1, tiles)
    loss_v[...] = jnp.sum(loss_all[0:3, 0:1], axis=0, keepdims=True)
    hand(2, coef_v, coef_out)
    hand(3, loss_v, loss_out)

    for cp in [qc, q_cp, i_cp, ic, s1c, s1, s2, s2c, bc, b_cp, s4, s5, s6, c1] + c2 + [c5, c6, c6c]:
        cp.wait_send()
    for cp in outs:
        cp.wait()


def hand_out(loss, coef, gh, ghead, ggain, loss_o, coef_o, gh_o, ghead_o, ggain_o, sems):
    rows = gh.shape[0] // 4
    pairs = [(gh.at[pl.ds(n * rows, rows)], gh_o.at[pl.ds(n * rows, rows)]) for n in range(4)]
    pairs += [(ghead, ghead_o), (coef, coef_o), (ggain, ggain_o), (loss, loss_o)]
    cps = [pltpu.make_async_copy(a, b, sems.at[n]) for n, (a, b) in enumerate(pairs)]
    for cp in cps:
        cp.start()
    for cp in cps:
        cp.wait()


def on_device(hidden, gain, head_weight, lengths, battles):
    toks, dl = hidden.shape
    models = head_weight.shape[0]
    prompts = lengths.shape[0]
    n_battles = battles.shape[0]
    tiles = -(-models // 16)
    wide = 16 * tiles
    blk = min(512, toks)
    levels = ZL.bit_length() - 1
    sem = pltpu.SemaphoreType.DMA
    hbm = pl.BlockSpec(memory_space=pl.ANY)
    V = pltpu.VMEM
    kinds = (
        ((1, 1), F32), ((models, prompts), F32), ((toks, dl), BF16), ((models, dl), F32), ((1, dl), F32)
    )
    operands = [hidden, gain.reshape(1, dl), head_weight, lengths.reshape(1, prompts), battles.T]
    operands = [pltpu.with_memory_space_constraint(a, pltpu.HBM) for a in operands]
    results = pl.pallas_call(
        functools.partial(kernel, models, float(dl * F), float(n_battles), blk),
        out_shape=tuple(pltpu.VMEM(*k) for k in kinds),
        in_specs=[hbm] * 5,
        out_specs=(hbm,) * 5,
        scratch_shapes=[
            V((toks, dl), BF16), V((1, dl), F32), V((models, dl), BF16),
            V((1, prompts), jnp.int32), V((2, n_battles), jnp.int32),
            V((wide, dl), BF16), V((wide, dl), BF16),
            V((toks, prompts), BF16), V((2 * PAIRS, toks), F32), V((wide, toks), F32),
            V((ZL, NC, 16, toks), BF16), V((toks, dl), BF16),
            V((1, 1), F32), V((models, prompts), F32), V((models, dl), F32), V((1, dl), F32),
            V((NC, ZL, 1, LANES), F32), *[V((ZL, 1, LANES), F32)] * 3, V((NC, ZL, 1, LANES), F32),
            V((NC, ZL, 8, LANES), F32), *[V((ZL, 8, LANES), F32)] * 3, V((NC, ZL, 8, LANES), F32),
            *[V((1, LANES), F32)] * 3, V((ZL, 1, LANES), F32),
            V((wide, toks), BF16), V((XY, 16, dl), F32), V((XY, 16, dl), BF16),
            V((XY, 16, dl), BF16), V((16, dl), F32), V((16, dl), F32), V((XY, 16, dl), BF16),
            V((ZL, 16, toks), BF16),
            V((XY, 16, prompts), BF16), V((NC, RING, 16, prompts), BF16),
            sem((4 + toks // blk,)), sem((4 + toks // blk,)),
            *[sem] * 28, sem((levels,)), sem((levels,)), *[sem] * 6,
        ]
        + [V((ZL >> (n + 1), 2, 16, toks), BF16) for n in range(levels)]
        + [V((ZL >> (n + 1), 16, toks), BF16) for n in range(levels)],
        compiler_params=pltpu.CompilerParams(
            collective_id=0, has_side_effects=True, vmem_limit_bytes=48 * 2**20
        ),
        name="head",
    )(*operands)
    loss, coef, gh, ghead, ggain = pl.pallas_call(
        hand_out,
        out_shape=tuple(pltpu.HBM(*k) for k in kinds),
        in_specs=[hbm] * 5,
        out_specs=(hbm,) * 5,
        scratch_shapes=[sem((8,))],
        compiler_params=pltpu.CompilerParams(vmem_limit_bytes=2**20),
        name="hand_out",
    )(*[pltpu.with_memory_space_constraint(a, pltpu.VMEM) for a in results])
    return loss.reshape(()), coef.T, gh, ghead, ggain.reshape(dl)


def solution(mesh):
    placed = (P("dp", "fsdp"), P("fsdp"), P(None, "fsdp"), P(), P())
    return jax.shard_map(
        on_device,
        mesh=mesh,
        in_specs=placed,
        out_specs=(P(), P(), P("dp", "fsdp"), P(None, "fsdp"), P("fsdp")),
        check_vma=False,
    )
```

```python
import functools

import jax
import jax.numpy as jnp
from jax import lax
from jax.experimental import pallas as pl
from jax.experimental.pallas import tpu as pltpu
from jax.sharding import PartitionSpec as P

Y, X, ZH, ZL, NC = 4, 4, 2, 8, 2
XY, F, DP, RING = Y * X, ZL * NC, Y * X * ZH, ZH * ZL
LANES = 128
PAIRS = 4
EPS = 1e-06
MESH = pl.DeviceIdType.MESH
F32, BF16 = jnp.float32, jnp.bfloat16


def nn(a, b):
    return lax.dot_general(a, b, (((1,), (0,)), ((), ())), preferred_element_type=F32)


def nt(a, b):
    return lax.dot_general(a, b, (((1,), (1,)), ((), ())), preferred_element_type=F32)


def tn(a, b):
    return lax.dot_general(a, b, (((0,), (0,)), ((), ())), preferred_element_type=F32)


def split3(x):
    hi = x.astype(BF16).astype(F32)
    mid = (x - hi).astype(BF16).astype(F32)
    return jnp.concatenate([hi, mid, x - hi - mid], axis=0).astype(BF16)


def join3(x):
    rows = x.shape[0] // 3
    return x[:rows] + x[rows : 2 * rows] + x[2 * rows :]


def kernel(
    models, width, n_battles, blk,
    hidden_hbm, gain_hbm, head_hbm, lens_hbm, battles_hbm,
    loss_out, coef_out, gh_out, ghead_out, ggain_out,
    hid, gain_v, head_v, lens_v, bat_v, wp, wpad, members, ids, raw, raw16, out_v,
    loss_v, coef_v, ghead_v, ggain_v,
    q_send, q_core, q_pair, q_recv, i_all, s1_send, s1_core, s1_pair, s1_recv, s2_all,
    b_send, b_core, b_sum, b_recv, g_t, g_tile, g_send, s4_recv,
    s5_send, s5_recv, ag, c1_recv, c5_all, ctab,
    load_sem, out_sem, qc_ss, qc_rs, q_ss, q_rs, i_ss, i_rs, ic_ss, ic_rs,
    s1c_ss, s1c_rs, s1_ss, s1_rs, s2_ss, s2_rs, s2c_ss, s2c_rs, bc_ss, bc_rs, b_ss, b_rs, s4_ss, s4_rs,
    s5_ss, s5_rs, s6_ss, s6_rs, c1_ss, c1_rs, c2_ss, c2_rs, c5_ss, c5_rs, c6_ss, c6_rs, c6c_ss, c6c_rs,
    *halves,
):
    toks, dl = hid.shape
    prompts = members.shape[1]
    tiles = -(-models // 16)
    levels = len(halves) // 2
    half, half_recv = halves[:levels], halves[levels:]
    dp = lax.axis_index("dp")
    f = lax.axis_index("fsdp")
    xy, zh = dp // ZH, dp % ZH
    y, x = xy // X, xy % X
    zl, c = f // NC, f % NC
    base = dp * toks

    def ring_peer(k):
        return lax.rem(zh * ZL + zl + k, RING)

    def ring_dev(r):
        return (xy * ZH + r // ZL, (r % ZL) * NC + c)

    def ring_slot(r):
        return lax.rem(zh * ZL + zl + RING - r, RING)

    def z_peer(k):
        return lax.rem(zl + k, ZL)

    def xy_peer(k):
        return lax.rem(y + k // X, Y) * X + lax.rem(x + k % X, X)

    def xy_dev(q):
        return (q * ZH + zh, f)

    core_dev = (dp, zl * NC + (1 - c))
    zh_dev = (xy * ZH + (1 - zh), f)
    dp_next, dp_prev = lax.rem(dp + 1, DP), lax.rem(dp + DP - 1, DP)

    barrier = pltpu.get_barrier_semaphore()
    partners = [core_dev] + [(dp, z_peer(k) * NC + c) for k in range(1, ZL)]
    partners += [xy_dev(xy_peer(k)) for k in range(1, XY)]
    partners += [((xy * ZH + (1 - zh)), r * NC + c) for r in range(ZL)]
    partners += [(dp_prev if r >= ZL // 2 else dp_next, r * NC + c) for r in range(ZL)]
    for dev in partners[::-1]:
        pl.semaphore_signal(barrier, inc=1, device_id=dev, device_id_type=MESH)

    loads = [
        pltpu.make_async_copy(lens_hbm, lens_v, load_sem.at[0]),
        pltpu.make_async_copy(battles_hbm, bat_v, load_sem.at[1]),
        pltpu.make_async_copy(gain_hbm, gain_v, load_sem.at[2]),
        pltpu.make_async_copy(head_hbm, head_v, load_sem.at[3]),
    ]
    n_blk = toks // blk
    for i in range(n_blk):
        rows = pl.ds(i * blk, blk)
        loads.append(pltpu.make_async_copy(hidden_hbm.at[rows], hid.at[rows], load_sem.at[4 + i]))
    for cp in loads:
        cp.start()

    loads[0].wait()
    lens = jnp.broadcast_to(lens_v[...], (8, prompts))
    len_hi = lens // 32
    len_lo = lens - len_hi * 32
    upto = (
        lax.broadcasted_iota(jnp.int32, (prompts, prompts), 0)
        <= lax.broadcasted_iota(jnp.int32, (prompts, prompts), 1)
    ).astype(F32).astype(BF16)
    ends = (32.0 * nn(len_hi.astype(F32).astype(BF16), upto) + nn(len_lo.astype(F32).astype(BF16), upto))[:1]
    ends = ends.astype(jnp.int32)
    lens = lens[:1]
    starts = ends - lens
    lens_f = lens.astype(F32)
    at_prev = ((starts < base) & (ends > base)).astype(F32)
    at_next = ((starts < base + toks) & (ends > base + toks)).astype(F32)
    here = jnp.minimum(ends, base + toks) - jnp.maximum(starts, base)
    here = jnp.maximum(here, 0).astype(F32)
    first, last = starts // toks, (ends - 1) // toks
    in_first = jnp.where(first == last, lens, last * toks - starts)
    in_low = jnp.where(first % ZH == 0, in_first, lens - in_first)
    owned = ((ends > base) & (ends <= base + toks)).astype(F32)
    before_end = jnp.sum(at_prev * ends.astype(F32), axis=1, keepdims=True)
    from_start = jnp.sum(at_next * starts.astype(F32), axis=1, keepdims=True)
    from_start = jnp.where(jnp.sum(at_next, axis=1, keepdims=True) > 0.0, from_start, 2.0**30)

    loads[2].wait()
    loads[3].wait()
    wide = 16 * tiles
    head_f = head_v[...].astype(F32)
    if wide > models:
        head_f = jnp.concatenate([head_f, jnp.zeros((wide - models, dl), F32)], axis=0)
    wpad[...] = head_f.astype(BF16)
    wp[...] = (head_f * gain_v[...]).astype(BF16)

    def remote(src, dst, ss, rs, dev):
        cp = pltpu.make_async_remote_copy(
            src_ref=src, dst_ref=dst, send_sem=ss, recv_sem=rs, device_id=dev, device_id_type=MESH
        )
        cp.start()
        return cp

    def scatter(src, dst, ss, rs, peer, dev):
        for k in range(1, dst.shape[0]):
            remote(src.at[peer(k)], dst.at[k], ss, rs, dev(peer(k)))
        rest = dst.at[pl.ds(1, dst.shape[0] - 1)]
        return pltpu.make_async_remote_copy(
            src_ref=rest, dst_ref=rest, send_sem=ss, recv_sem=rs, device_id=dev(peer(1)), device_id_type=MESH
        )

    def gather(buf, ss, rs, peer, dev):
        for k in range(1, buf.shape[0]):
            remote(buf.at[0], buf.at[k], ss, rs, dev(peer(k)))
        rest = buf.at[pl.ds(1, buf.shape[0] - 1)]
        return pltpu.make_async_remote_copy(
            src_ref=rest, dst_ref=rest, send_sem=ss, recv_sem=rs, device_id=dev(peer(1)), device_id_type=MESH
        )

    def z_dev(r):
        return (dp, r * NC + c)

    def z_slot(r):
        return lax.rem(zl + ZL - r, ZL)

    def xy_slot(q):
        return lax.rem(y + Y - q // X, Y) * X + lax.rem(x + X - q % X, X)

    for t in range(tiles, ZL * NC):
        raw16[t // NC, t % NC] = jnp.zeros((16, toks), BF16)
    for i in range(n_blk):
        loads[4 + i].wait()
        rows = pl.ds(i * blk, blk)
        block = nt(wp[...], hid[rows, :])
        raw[:, rows] = block
        for t in range(tiles):
            raw16[t // NC, t % NC, :, rows] = block[16 * t : 16 * t + 16].astype(BF16)

    bits = [(zl >> n) % 2 for n in range(levels)]

    def halve(n):
        step = 1 << n
        peer = (zl + step - 2 * step * bits[n]) * NC + c
        return remote(half[n].at[:, 1 - bits[n]], half_recv[n], c2_ss.at[n], c2_rs.at[n], (dp, peer))

    def fold(n):
        for j in range(half_recv[n].shape[0]):
            total = half[n][j, bits[n]].astype(F32) + half_recv[n][j].astype(F32)
            half[n + 1][j // 2, j % 2] = total.astype(BF16)

    for i in range(n_blk):
        pos = base + i * blk + lax.broadcasted_iota(jnp.int32, (blk, prompts), 0)
        inside = (pos >= starts) & (pos < ends)
        members[pl.ds(i * blk, blk), :] = inside.astype(F32).astype(BF16)
    loads[1].wait()
    n_bat = bat_v.shape[1]
    bat_row = lax.broadcasted_iota(jnp.int32, (2 * PAIRS, n_bat), 0)
    bat_lane = lax.broadcasted_iota(jnp.int32, (2 * PAIRS, n_bat), 1)
    bat = jnp.where(bat_row < PAIRS, bat_v[0:1, :], bat_v[1:2, :])
    bat = jnp.where(bat_lane % PAIRS == bat_row % PAIRS, bat, 0)
    judged = lax.broadcasted_iota(jnp.int32, (n_bat, prompts), 0) // PAIRS
    judged = judged == lax.broadcasted_iota(jnp.int32, (n_bat, prompts), 1)
    bat = nn(bat.astype(F32).astype(BF16), judged.astype(F32).astype(BF16))
    ids[...] = nt(bat.astype(BF16), members[...])

    ones_l = jnp.ones((8, LANES), BF16)
    for i in range(n_blk):
        hf = hid[pl.ds(i * blk, blk), :].astype(F32)
        sq = hf * hf
        part = sq[:, :LANES]
        for j in range(1, dl // LANES):
            part = part + sq[:, j * LANES : (j + 1) * LANES]
        part_hi = part.astype(BF16)
        part_lo = (part - part_hi.astype(F32)).astype(BF16)
        sumsq = nt(ones_l, part_hi) + nt(ones_l, part_lo)
        for b in range(blk // LANES):
            dest = i * (blk // LANES) + b
            q_send[dest % NC, dest // NC] = sumsq[0:1, b * LANES : (b + 1) * LANES]
    model_of = lax.broadcasted_iota(jnp.int32, (wide, LANES), 0).astype(F32)
    for b in range(toks // LANES):
        lanes = slice(b * LANES, (b + 1) * LANES)
        id_blk = ids[:, lanes]
        found = [jnp.zeros((8, LANES), F32) for _ in range(2 * PAIRS)]
        for t in range(wide // 8):
            rows = slice(8 * t, 8 * t + 8)
            block, number = raw[rows, lanes], model_of[rows]
            found = [jnp.where(number == id_blk[j : j + 1], block, found[j]) for j in range(2 * PAIRS)]
        picked = [jnp.sum(one, axis=0, keepdims=True) for one in found]
        s1_send[b % NC, b // NC] = jnp.concatenate(picked, axis=0)

    pl.semaphore_wait(barrier, len(partners))
    s1c = remote(s1_send.at[1 - c], s1_core, s1c_ss, s1c_rs, core_dev)
    qc = remote(q_send.at[1 - c], q_core, qc_ss, qc_rs, core_dev)
    c1 = remote(raw16.at[:, 1 - c], c1_recv, c1_ss, c1_rs, (dp, zl * NC + (1 - c)))

    s1c.wait_recv()
    s1_pair[...] = s1_send[c] + s1_core[...]
    s1 = scatter(s1_pair, s1_recv, s1_ss, s1_rs, z_peer, z_dev)
    qc.wait_recv()
    q_pair[...] = q_send[c] + q_core[...]
    q_cp = scatter(q_pair, q_recv, q_ss, q_rs, z_peer, z_dev)
    c1.wait_recv()
    for k in range(ZL):
        half[0][k // 2, k % 2] = (raw16[k, c].astype(F32) + c1_recv[k].astype(F32)).astype(BF16)
    c2 = [halve(0)]


    q_cp.wait_recv()
    acc = q_pair[zl]
    for k in range(1, ZL):
        acc = acc + q_recv[k]
    inv_own = lax.rsqrt(acc / width + EPS)
    i_all[c, 0] = inv_own
    s1.wait_recv()
    acc = s1_pair[zl]
    for k in range(1, ZL):
        acc = acc + s1_recv[k]
    own = acc * inv_own
    s2_all[c, 0] = own
    s2 = gather(s2_all.at[c], s2_ss, s2_rs, z_peer, z_dev)
    i_cp = gather(i_all.at[c], i_ss, i_rs, z_peer, z_dev)

    late = f >= F // 2
    pos = base + f * LANES + lax.broadcasted_iota(jnp.int32, (8, LANES), 1)
    pos = pos.astype(F32)
    crossing = jnp.where(late, (pos >= from_start).astype(F32), (pos < before_end).astype(F32))
    column = jnp.sum(jnp.exp(own) * crossing, axis=1, keepdims=True)
    eye = lax.broadcasted_iota(jnp.int32, (8, LANES), 0) == lax.broadcasted_iota(jnp.int32, (8, LANES), 1)
    b_send[...] = jnp.sum(jnp.where(eye, column, 0.0), axis=0, keepdims=True)
    to_dp = jnp.where(late, dp_next, dp_prev)
    bc = remote(b_send, b_core, bc_ss, bc_rs, core_dev)
    bc.wait_recv()
    b_sum[...] = b_send[...] + b_core[...]
    for k in range(ZL):
        remote(b_sum, b_recv.at[zl], b_ss, b_rs, (to_dp, z_peer(k) * NC + c))
    b_cp = pltpu.make_async_remote_copy(
        src_ref=b_recv, dst_ref=b_recv, send_sem=b_ss, recv_sem=b_rs,
        device_id=(to_dp, f), device_id_type=MESH,
    )

    c2[0].wait_recv()
    fold(0)
    c2.append(halve(1))

    s2.wait_recv()
    s2c = remote(s2_all.at[c], s2_all.at[c], s2c_ss, s2c_rs, core_dev)
    i_cp.wait_recv()
    ic = remote(i_all.at[c], i_all.at[c], ic_ss, ic_rs, core_dev)
    for n in range(1, levels - 1):
        c2[n].wait_recv()
        fold(n)
        c2.append(halve(n + 1))

    s2c.wait_recv()
    ic.wait_recv()
    logits = jnp.concatenate([s2_all[r % NC, z_slot(r // NC)] for r in range(F)], axis=1)
    inv = jnp.concatenate([i_all[r % NC, z_slot(r // NC)] for r in range(F)], axis=1)
    exps = jnp.exp(logits)
    pooled = join3(nn(split3(exps), members[...]))
    b_cp.wait_recv()

    def column_of(rs):
        row = b_recv[rs[0]]
        for r in rs[1:]:
            row = row + b_recv[r]
        return jnp.sum(jnp.where(eye, row, 0.0), axis=1, keepdims=True)

    from_prev = column_of(range(ZL // 2, ZL))
    from_next = column_of(range(ZL // 2))
    pooled = pooled + from_prev * at_prev + from_next * at_next
    pooled = jnp.where(pooled > 0.0, pooled, 1.0)
    coef = jnp.log(pooled / lens_f)
    other = jnp.concatenate([coef[PAIRS:], coef[:PAIRS]], axis=0)
    row_of = lax.broadcasted_iota(jnp.int32, (8, prompts), 0)
    sign = jnp.where(row_of < PAIRS, -1.0, 1.0)
    margin = sign * (coef - other)
    ratio = sign * (1.0 / (1.0 + jnp.exp(-margin))) / n_battles / pooled
    grads = exps * join3(nt(split3(ratio), members[...]))
    slope = jnp.sum(grads * logits, axis=0, keepdims=True) * inv * inv / width
    grads = grads * inv
    model_16 = model_of.astype(BF16)

    for b in range(toks // LANES):
        lanes = slice(b * LANES, (b + 1) * LANES)
        id_blk = ids[:, lanes]
        g_blk = grads[:, lanes]
        same = jnp.zeros((8, LANES), F32)
        for j in range(2 * PAIRS):
            same = same + jnp.where(id_blk == id_blk[j : j + 1], g_blk[j : j + 1], 0.0)
        one_id = [jnp.broadcast_to(id_blk[j : j + 1], (16, LANES)).astype(BF16) for j in range(2 * PAIRS)]
        one_g = [jnp.broadcast_to(same[j : j + 1], (16, LANES)).astype(BF16) for j in range(2 * PAIRS)]
        for t in range(wide // 16):
            rows = slice(16 * t, 16 * t + 16)
            full = jnp.zeros((16, LANES), BF16)
            for j in range(2 * PAIRS):
                full = jnp.where(model_16[rows] == one_id[j], one_g[j], full)
            g_t[rows, lanes] = full
    head_part = nn(g_t[...], hid[...])
    for t in range(tiles):
        g_tile[t] = head_part[16 * t : 16 * t + 16]
        g_send[t] = head_part[16 * t : 16 * t + 16].astype(BF16)
    for t in range(tiles, XY):
        g_tile[t] = jnp.zeros((16, dl), F32)
        g_send[t] = jnp.zeros((16, dl), BF16)
    s4 = scatter(g_send, s4_recv, s4_ss, s4_rs, xy_peer, xy_dev)

    softplus = jnp.maximum(margin, 0.0) + jnp.log1p(jnp.exp(-jnp.abs(margin)))
    loss_part = jnp.sum(jnp.where(row_of < PAIRS, softplus * owned, 0.0)) / n_battles

    c2[-1].wait_recv()
    tile = half[-1][0, bits[-1]].astype(F32) + half_recv[-1][0].astype(F32)
    c_blk = join3(nn(split3(jnp.exp(tile * inv)), members[...]))
    local = jnp.log(jnp.where(here > 0.0, c_blk, 1.0) / jnp.maximum(here, 1.0))
    crow = lax.broadcasted_iota(jnp.int32, (16, prompts), 0)

    def loss_rows(total):
        hi = total.astype(BF16).astype(F32)
        mid = (total - hi).astype(BF16).astype(F32)
        return jnp.where(crow == 0, hi, jnp.where(crow == 1, mid, jnp.where(crow == 2, total - hi - mid, 0.0)))

    loss_part = jnp.broadcast_to(loss_part, (16, prompts))
    mine = jnp.where(f == tiles, loss_rows(loss_part), local).astype(BF16)
    c5_all[0] = mine
    c5 = gather(c5_all, c5_ss, c5_rs, xy_peer, xy_dev)

    s4.wait_recv()
    total = g_tile[xy]
    for k in range(1, XY):
        total = total + s4_recv[k].astype(F32)
    s5_send[...] = total
    s5 = remote(s5_send, s5_recv, s5_ss, s5_rs, zh_dev)

    c5.wait_recv()
    csum = c5_all[xy_slot(0)].astype(F32)
    for q in range(1, XY):
        csum = csum + c5_all[xy_slot(q)].astype(F32)
    csum = jnp.where(f == tiles, loss_rows(csum[0:1] + csum[1:2] + csum[2:3]), csum)
    ctab[c, 0] = csum.astype(BF16)
    c6 = gather(ctab.at[c], c6_ss, c6_rs, ring_peer, ring_dev)

    c_rows = lax.broadcasted_iota(jnp.int32, (16, toks), 0)
    slope_hi = slope.astype(BF16).astype(F32)
    slope_lo = slope - slope_hi
    slope3 = jnp.where(c_rows == 0, slope_hi, jnp.where(c_rows == 1, slope_lo, 0.0)).astype(BF16)
    ones_w = jnp.ones((16, dl), BF16)
    outs = []
    for i in range(n_blk):
        rows = pl.ds(i * blk, blk)
        gn = tn(g_t[:, rows], wpad[...])
        cb = tn(slope3[:, i * blk : (i + 1) * blk], ones_w)
        out_v[rows, :] = (gain_v[...] * gn - hid[rows, :].astype(F32) * cb).astype(BF16)
        cp = pltpu.make_async_copy(out_v.at[rows], gh_out.at[rows], out_sem.at[i])
        cp.start()
        outs.append(cp)

    s5.wait_recv()
    ag[0] = (s5_send[...] + s5_recv[...]).astype(BF16)
    s6 = gather(ag, s6_ss, s6_rs, xy_peer, xy_dev)

    def hand(n, src, dst):
        cp = pltpu.make_async_copy(src, dst, out_sem.at[n_blk + n])
        cp.start()
        outs.append(cp)

    c6.wait_recv()
    c6c = remote(ctab.at[c], ctab.at[c], c6c_ss, c6c_rs, core_dev)
    s6.wait_recv()
    whole = jnp.concatenate([ag[xy_slot(t)].astype(F32) for t in range(tiles)], axis=0)
    ghead_v[...] = (gain_v[...] * whole)[:models]
    ggain_v[...] = jnp.sum(wpad[...].astype(F32) * whole, axis=0, keepdims=True)
    hand(0, ghead_v, ghead_out)
    hand(1, ggain_v, ggain_out)

    c6c.wait_recv()

    def slot_of(half_at, t):
        return ctab[t % NC, ring_slot(half_at * ZL + t // NC)].astype(F32)

    low, high = (jnp.concatenate([slot_of(n, t) for t in range(tiles)], axis=0) for n in range(ZH))
    low_share = in_low.astype(F32) / lens_f
    high_share = (lens - in_low).astype(F32) / lens_f
    table = jnp.log(low_share * jnp.exp(low) + high_share * jnp.exp(high))
    table = jnp.where(in_low == lens, low, jnp.where(in_low == 0, high, table))
    coef_v[...] = table[:models]
    loss_all = slot_of(0, tiles) + slot_of(1, tiles)
    loss_v[...] = jnp.sum(loss_all[0:3, 0:1], axis=0, keepdims=True)
    hand(2, coef_v, coef_out)
    hand(3, loss_v, loss_out)

    for cp in [qc, q_cp, i_cp, ic, s1c, s1, s2, s2c, bc, b_cp, s4, s5, s6, c1] + c2 + [c5, c6, c6c]:
        cp.wait_send()
    for cp in outs:
        cp.wait()


def hand_out(loss, coef, gh, ghead, ggain, loss_o, coef_o, gh_o, ghead_o, ggain_o, sems):
    rows = gh.shape[0] // 4
    pairs = [(gh.at[pl.ds(n * rows, rows)], gh_o.at[pl.ds(n * rows, rows)]) for n in range(4)]
    pairs += [(ghead, ghead_o), (coef, coef_o), (ggain, ggain_o), (loss, loss_o)]
    cps = [pltpu.make_async_copy(a, b, sems.at[n]) for n, (a, b) in enumerate(pairs)]
    for cp in cps:
        cp.start()
    for cp in cps:
        cp.wait()


def on_device(hidden, gain, head_weight, lengths, battles):
    toks, dl = hidden.shape
    models = head_weight.shape[0]
    prompts = lengths.shape[0]
    n_battles = battles.shape[0]
    tiles = -(-models // 16)
    wide = 16 * tiles
    blk = min(512, toks)
    levels = ZL.bit_length() - 1
    sem = pltpu.SemaphoreType.DMA
    hbm = pl.BlockSpec(memory_space=pl.ANY)
    V = pltpu.VMEM
    kinds = (
        ((1, 1), F32), ((models, prompts), F32), ((toks, dl), BF16), ((models, dl), F32), ((1, dl), F32)
    )
    operands = [hidden, gain.reshape(1, dl), head_weight, lengths.reshape(1, prompts), battles.T]
    operands = [pltpu.with_memory_space_constraint(a, pltpu.HBM) for a in operands]
    results = pl.pallas_call(
        functools.partial(kernel, models, float(dl * F), float(n_battles), blk),
        out_shape=tuple(pltpu.VMEM(*k) for k in kinds),
        in_specs=[hbm] * 5,
        out_specs=(hbm,) * 5,
        scratch_shapes=[
            V((toks, dl), BF16), V((1, dl), F32), V((models, dl), BF16),
            V((1, prompts), jnp.int32), V((2, n_battles), jnp.int32),
            V((wide, dl), BF16), V((wide, dl), BF16),
            V((toks, prompts), BF16), V((2 * PAIRS, toks), F32), V((wide, toks), F32),
            V((ZL, NC, 16, toks), BF16), V((toks, dl), BF16),
            V((1, 1), F32), V((models, prompts), F32), V((models, dl), F32), V((1, dl), F32),
            V((NC, ZL, 1, LANES), F32), *[V((ZL, 1, LANES), F32)] * 3, V((NC, ZL, 1, LANES), F32),
            V((NC, ZL, 8, LANES), F32), *[V((ZL, 8, LANES), F32)] * 3, V((NC, ZL, 8, LANES), F32),
            *[V((1, LANES), F32)] * 3, V((ZL, 1, LANES), F32),
            V((wide, toks), BF16), V((XY, 16, dl), F32), V((XY, 16, dl), BF16),
            V((XY, 16, dl), BF16), V((16, dl), F32), V((16, dl), F32), V((XY, 16, dl), BF16),
            V((ZL, 16, toks), BF16),
            V((XY, 16, prompts), BF16), V((NC, RING, 16, prompts), BF16),
            sem((4 + toks // blk,)), sem((4 + toks // blk,)),
            *[sem] * 28, sem((levels,)), sem((levels,)), *[sem] * 6,
        ]
        + [V((ZL >> (n + 1), 2, 16, toks), BF16) for n in range(levels)]
        + [V((ZL >> (n + 1), 16, toks), BF16) for n in range(levels)],
        compiler_params=pltpu.CompilerParams(
            collective_id=0, has_side_effects=True, vmem_limit_bytes=48 * 2**20
        ),
        name="head",
    )(*operands)
    loss, coef, gh, ghead, ggain = pl.pallas_call(
        hand_out,
        out_shape=tuple(pltpu.HBM(*k) for k in kinds),
        in_specs=[hbm] * 5,
        out_specs=(hbm,) * 5,
        scratch_shapes=[sem((8,))],
        compiler_params=pltpu.CompilerParams(vmem_limit_bytes=2**20),
        name="hand_out",
    )(*[pltpu.with_memory_space_constraint(a, pltpu.VMEM) for a in results])
    return loss.reshape(()), coef.T, gh, ghead, ggain.reshape(dl)


def solution(mesh):
    placed = (P("dp", "fsdp"), P("fsdp"), P(None, "fsdp"), P(), P())
    return jax.shard_map(
        on_device,
        mesh=mesh,
        in_specs=placed,
        out_specs=(P(), P(), P("dp", "fsdp"), P(None, "fsdp"), P("fsdp")),
        check_vma=False,
    )
```
